256 devices in a mesh: mem: 8 (over x, core), band: 32 (over y, z).
Axes of the slice: x: 4, y: 4, z: 8, core: 2. Of those that a mesh axis runs over, the one named last changes fastest.
Arguments:
- control: bfloat16 [128, 2, 1536, 768], P('mem', None, 'band'), may hold values from -11 to 11
- member_pert: bfloat16 [128, 65536], P('mem', 'band'), may hold values from -6 to 6
- obs_weight: float32 [65536], P('band'), may hold values from 0.5 to 2
- obs_band: int32 [65536, 1], P('band'), may hold values from 0 to 31; in each aligned block of 2048 rows (0 to 2047, 2048 to 4095, ...) at most 128 rows name the same one
- obs_cell: int32 [65536], P('band'), may hold values from 0 to 73727
- length_x: float32 [2], replicated, may hold values from 30 to 120
- length_y: float32 [2], replicated, may hold values from 30 to 120
Outputs:
- gradient: float32 [128, 2, 1536, 768], P('mem', None, 'band')
- gradient_dot: float32 [], replicated
The draws below stay inside these ranges and needn't reach their ends.
Inputs may be any that keep to these rules, and one draw needn't show every extreme that they name: `obs_band`: in each aligned block of 2048 rows (the rows of one band), at most 128 rows name the same band.
All inputs are finite; a program needn't handle non-finite values.
Results may differ from the reference program's by a relative error of at most 0.024.
Values may be sent and summed in bfloat16 or wider, within the bound.
No kernel may reach another device: no remote copies, remote signals or barrier semaphores. Data moves between devices by JAX's collectives and lax.ppermute only.
A program may use at most 192 MiB of HBM per device.

```python
import math
import jax
import jax.numpy as jnp
import numpy as np
from jax import lax

NX = 1536
NY = 768
LEV = 2
OBS_DEV = 2048
MEMBERS = 128
NY_LOC = 24
CELLS = 73728
OBS = 65536
CAP = 128
N_BAND = 32


def draw_control(key, part):
    member_idx = jnp.arange(MEMBERS, dtype=jnp.float32)[:, None, None, None]
    column_idx = jnp.arange(NX, dtype=jnp.float32)[None, None, :, None]
    fraction = (member_idx * NX + column_idx) / (MEMBERS * NX)
    base = jnp.clip(jax.random.normal(key, (MEMBERS, LEV, NX, NY), jnp.float32), -6.0, 6.0)
    scale = jnp.sqrt(1.0 + 2.0 * fraction)
    return (base * scale).astype(jnp.bfloat16)


def set_ends(entries, rng, least, largest):
    spot = [jax.random.randint(jax.random.fold_in(rng, axis), (), 0, length) for axis, length in enumerate(entries.shape)]
    longest = entries.shape.index(max(entries.shape))
    next_to = spot[:longest] + [(spot[longest] + 1) % entries.shape[longest]] + spot[longest + 1:]
    return entries.at[tuple(spot)].set(least).at[tuple(next_to)].set(largest)


def shard_levels(stream_key, shape, shards, least, top_value):
    loudness = 1.0
    for dim, shards_of in shards:
        draws = jax.random.uniform(jax.random.fold_in(jax.random.fold_in(stream_key, 6), dim), (shards_of,), jnp.float32, least / len(shards), top_value / len(shards))
        loudness = loudness * jnp.repeat(jnp.exp(draws), shape[dim] // shards_of).reshape((-1,) + (1,) * (len(shape) - 1 - dim))
    return loudness


def deal_out(stream_key, own, number, rows, count, top, limit, lean):
    ranking = jax.random.permutation(stream_key, count)
    crowded, usual = shares(count, rows * top, limit, lean, True), shares(count, rows * top, limit, lean, False)
    places = jnp.arange(count)

    def named(sizes, rotation):
        used = int((sizes > 0).sum())
        fixed = max(1, used // 4)
        shifted = fixed + (places - fixed + rotation * (used - fixed)) % max(1, count - fixed)
        return jnp.zeros((count,), jnp.int32).at[ranking[jnp.where(places < fixed, places, shifted)]].set(jnp.asarray(sizes, jnp.int32))

    sizes = jnp.where(number % 4 == 0, named(crowded, number // 4), named(usual, number - number // 4 - 1))
    mixed = jax.random.permutation(jax.random.fold_in(own, 3), count)
    donor, taker = mixed[0:count // 2 * 2:2], mixed[1:count // 2 * 2:2]
    margin = jnp.minimum(sizes[donor] - 1, limit - sizes[taker]) // 2
    margin = jnp.where((donor == ranking[0]) | (taker == ranking[0]) | (sizes[taker] == 0), 0, jnp.maximum(margin, 0))
    shifted = jax.random.randint(jax.random.fold_in(own, 4), (count // 2,), 0, 1 << 20) % (margin + 1)
    sizes = sizes.at[donor].add(-shifted).at[taker].add(shifted)
    labels = jnp.searchsorted(jnp.cumsum(sizes), jnp.arange(rows * top), side="right").astype(jnp.int32)
    table = labels.reshape(top, rows).T
    table = table[jax.random.permutation(jax.random.fold_in(own, 1), rows)]
    rotation = jax.random.randint(jax.random.fold_in(own, 2), (rows, 1), 0, top)
    return jnp.take_along_axis(table, (jnp.arange(top)[None, :] + rotation) % top, axis=1)


def shares(number_of, total, bound, skew, full):
    weights = [(1 << 20) // math.isqrt(standing ** skew) + 1 for standing in range(1, number_of + 1)]
    largest = bound if full else min(bound, max(-(-total // number_of), total * weights[0] // sum(weights)))
    least = 1 if total - largest >= number_of - 1 else 0
    holding, surplus = [largest] + [least] * (number_of - 1), total - largest - least * (number_of - 1)
    while surplus > 0:
        movable = [i for i in range(1, number_of) if holding[i] < largest] or [i for i in range(1, number_of) if holding[i] < bound]
        mass, remaining = sum([weights[i] for i in movable]), surplus
        for i in movable:
            addition = min(bound - holding[i], max(1, remaining * weights[i] // mass), surplus)
            holding[i] = holding[i] + addition
            surplus = surplus - addition
    return np.array(holding)


def centred(own_key, shape, scale, limit, pieces=(), kind=jnp.bfloat16):
    gain = shard_levels(own_key, shape, pieces, -0.22, 0.18) if pieces else 1.0
    result = jax.random.normal(own_key, shape, jnp.float32) * scale * gain
    return jnp.minimum(jnp.maximum(result, -limit), limit).astype(kind)


def setup_inputs(seed: int = 0) -> dict:
    streams_of = jax.random.split(jax.random.key(seed), 8)
    control = draw_control(jax.random.fold_in(streams_of[7], 71), 0)
    member_pert = centred(streams_of[1], (MEMBERS, OBS), 1.0, 6.0, ((0, 8), (1, 32)))
    obs_weight = jnp.clip(jnp.exp(math.log(2.0) - 1.3862944 * jax.random.uniform(streams_of[2], (OBS,), jnp.float32) ** shard_levels(streams_of[2], (OBS,), ((0, 32),), -0.2, 0.2)), 0.5, 2.0)
    obs_band_keys = jax.random.split(jax.random.fold_in(streams_of[3], 1), OBS // OBS_DEV)
    obs_band_turns = jax.random.permutation(jax.random.fold_in(streams_of[3], 3), OBS // OBS_DEV)
    obs_band = jax.vmap(lambda own, number: deal_out(jax.random.fold_in(streams_of[3], 2), own, number, OBS_DEV, N_BAND, 1, CAP, 2))(obs_band_keys, obs_band_turns).reshape((OBS, 1))
    obs_cell = set_ends(jax.random.randint(streams_of[4], (OBS,), 0, CELLS), jax.random.fold_in(streams_of[4], 1), 0, CELLS - 1).astype(jnp.int32)
    length_x = jnp.clip(jnp.exp(jax.random.uniform(streams_of[5], (LEV,), jnp.float32, math.log(30.0), math.log(120.0))), 30.0, 120.0)
    length_y = jnp.clip(jnp.exp(jax.random.uniform(streams_of[6], (LEV,), jnp.float32, math.log(30.0), math.log(120.0))), 30.0, 120.0)
    return {"control": control, "member_pert": member_pert, "obs_weight": obs_weight, "obs_band": obs_band, "obs_cell": obs_cell, "length_x": length_x, "length_y": length_y}


def kernels(lengths, length_n, periodic):
    offset = jnp.arange(length_n, dtype=jnp.int32)
    spread = jnp.abs(offset[:, None] - offset[None, :]).astype(jnp.float32)
    if periodic:
        spread = jnp.minimum(spread, length_n - spread)
    scale = 2.0 / jnp.sqrt(lengths)
    return (scale[:, None, None] * jnp.exp(-spread[None, :, :] / lengths[:, None, None])).astype(jnp.bfloat16)

def reference(control, member_pert, obs_weight, obs_band, obs_cell, length_x, length_y):
    plane = NY_LOC * NX
    target = obs_band[:, 0].astype(jnp.int32)
    level_of = obs_cell // plane
    in_plane = obs_cell % plane
    flat_cell = level_of * (NY * NX) + (target * NY_LOC + in_plane // NX) * NX + in_plane % NX
    payload = obs_weight[None, :] * member_pert.astype(jnp.float32)
    filter_x = kernels(length_x, NX, True)
    filter_y = kernels(length_y, NY, False)

    def one_member(inputs):
        payload_row, control_row = inputs
        grid_sum = jnp.zeros((LEV * NY * NX,), jnp.float32).at[flat_cell].add(payload_row)
        grid_sum = grid_sum.reshape(LEV, NY, NX).astype(jnp.bfloat16)
        zonal = jnp.einsum('lyx,lxw->lyw', grid_sum.astype(jnp.float32), filter_x.astype(jnp.float32)).astype(jnp.bfloat16)
        gradient = control_row.astype(jnp.float32) + jnp.einsum('lax,lya->lxy', zonal.astype(jnp.float32), filter_y.astype(jnp.float32))
        partial_value = jnp.sum(gradient * gradient)
        return (gradient, partial_value)
    gradient, partials = lax.map(one_member, (payload, control))
    gradient_dot = jnp.sum(partials) * (1.0 / (MEMBERS * LEV * NY * NX))
    return (gradient, gradient_dot)
```

```python
import math

import jax
import jax.numpy as jnp
from jax import lax
from jax.experimental import pallas as pl
from jax.experimental.pallas import tpu as pltpu
from jax.sharding import PartitionSpec as P

CAP = 128
ROWS = 32
F32 = jnp.float32
BF16 = jnp.bfloat16
VMEM_LIMIT = 56 * 1024 * 1024
LOG2E = 1.4426950408889634


def iota(shape, dim):
    return lax.broadcasted_iota(jnp.int32, shape, dim)


def dot_last(a, b):
    return lax.dot_general(a, b, (((1,), (1,)), ((), ())), preferred_element_type=F32)


def bucket_body(nx, band_ref, cell_ref, weight_ref, pert_ref, out_ref, slot_ref, data_ref):
    bands = out_ref.shape[0]
    members, obs = pert_ref.shape
    earlier = (iota((128, 128), 0) < iota((128, 128), 1)).astype(F32).astype(BF16)
    running = jnp.zeros((bands, 1), F32)
    for part in range(obs // 128):
        at = pl.ds(part * 128, 128)
        target = band_ref[:, at]
        named = (iota((bands, 128), 0) == target).astype(F32)
        before = jnp.dot(named.astype(BF16), earlier, preferred_element_type=F32)
        rank = jnp.sum(named * (before + running), axis=0, keepdims=True)
        slot_ref[:, at] = target * CAP + rank.astype(jnp.int32)
        running = running + jnp.sum(named, axis=1, keepdims=True)
    cell = cell_ref[...]
    row = ((cell.astype(F32) + 0.5) * (1.0 / nx)).astype(jnp.int32)
    col = cell - row * nx
    data_ref[:members, :] = (weight_ref[...] * pert_ref[...].astype(F32)).astype(BF16)
    pick = iota((ROWS - members, obs), 0)
    coords = jnp.where(pick == 0, row, jnp.where(pick == 1, col >> 8, jnp.where(pick == 2, col & 255, 0)))
    data_ref[members:, :] = coords.astype(F32).astype(BF16)

    def fill(dest, carry):
        slots = dest * CAP + iota((CAP, obs), 0)
        move = (slots == slot_ref[...]).astype(F32).astype(BF16)
        out_ref[dest] = dot_last(data_ref[...], move).astype(BF16)
        return carry

    lax.fori_loop(0, bands, fill, 0)


def zonal_body(nx, rows, length_ref, got_ref, out_ref, a_ref, obs_ref):
    srcs = got_ref.shape[0]
    tile = out_ref.shape[0]
    step = pl.program_id(0)
    members = a_ref.shape[0] // rows

    @pl.when(step == 0)
    def _():
        for src in range(srcs):
            at = pl.ds(src * CAP, CAP)
            got = got_ref[src].astype(F32)
            row = got[members : members + 1]
            length = jnp.where(row >= rows // 2, length_ref[1], length_ref[0])
            obs_ref[0:1, at] = got[members + 1 : members + 2] * 256.0 + got[members + 2 : members + 3]
            obs_ref[1:2, at] = LOG2E / length
            obs_ref[2:3, at] = 1.0 - (0.5 * LOG2E) * jnp.log(length)
            here = iota((rows, CAP), 0).astype(F32) == row
            for k in range(members):
                a_ref[k * rows : (k + 1) * rows, at] = jnp.where(here, got[k : k + 1], 0.0).astype(BF16)

    chunk = 512
    total = jnp.zeros((tile, a_ref.shape[0]), F32)
    for part in range(srcs * CAP // chunk):
        at = pl.ds(part * chunk, chunk)
        x = (iota((tile, chunk), 0) + step * tile).astype(F32)
        gap = jnp.abs(x - obs_ref[0:1, at])
        gap = jnp.minimum(gap, nx - gap)
        fx = jnp.exp2(obs_ref[2:3, at] - gap * obs_ref[1:2, at]).astype(BF16)
        total = total + dot_last(fx, a_ref[:, at])
    out_ref[...] = total.astype(BF16)


def final_body(got_ref, fy_ref, control_ref, out_ref, sum_ref, lhs_ref):
    bands, cols, lanes = got_ref.shape
    members, levels, _, ny = out_ref.shape
    rows = lanes // members
    for k in range(members):
        for b0 in range(0, bands, 8):
            lhs_ref[k * cols : (k + 1) * cols, b0 * rows : (b0 + 8) * rows] = jnp.concatenate(
                [got_ref[b, :, k * rows : (k + 1) * rows] for b in range(b0, b0 + 8)], axis=1
            )
    total = jnp.zeros((8, ny), F32)
    for k in range(members):
        for level in range(levels):
            value = jnp.dot(
                lhs_ref[k * cols : (k + 1) * cols, :],
                fy_ref[:, level * ny : (level + 1) * ny],
                preferred_element_type=F32,
            )
            value = value + control_ref[k, level].astype(F32)
            out_ref[k, level] = value
            total = total + jnp.sum((value * value).reshape(cols // 8, 8, ny), axis=0)

    @pl.when(pl.program_id(0) == 0)
    def _():
        sum_ref[...] = total

    @pl.when(pl.program_id(0) > 0)
    def _():
        sum_ref[...] = sum_ref[...] + total


def on_device(control, member_pert, obs_weight, obs_band, obs_cell, length_x, length_y):
    members, levels, x_block, ny = control.shape
    bands = lax.axis_size("band")
    groups = lax.axis_size("mem")
    ny_loc = ny // bands
    nx = x_block * bands
    obs = obs_cell.shape[0]
    rows = levels * ny_loc
    params = pltpu.CompilerParams(vmem_limit_bytes=VMEM_LIMIT)

    packed = pl.pallas_call(
        lambda *refs: bucket_body(nx, *refs),
        out_shape=jax.ShapeDtypeStruct((bands, ROWS, CAP), BF16),
        scratch_shapes=[pltpu.VMEM((1, obs), jnp.int32), pltpu.VMEM((ROWS, obs), BF16)],
        compiler_params=params,
        name="bucket",
    )(obs_band.reshape(1, obs), obs_cell.reshape(1, obs), obs_weight.reshape(1, obs), member_pert)
    got = lax.all_to_all(packed, "band", 0, 0, tiled=True)

    tile = 256
    zonal = pl.pallas_call(
        lambda *refs: zonal_body(nx, rows, *refs),
        grid=(nx // tile,),
        in_specs=[
            pl.BlockSpec(memory_space=pltpu.SMEM),
            pl.BlockSpec((bands, ROWS, CAP), lambda i: (0, 0, 0)),
        ],
        out_specs=pl.BlockSpec((tile, members * rows), lambda i: (i, 0)),
        out_shape=jax.ShapeDtypeStruct((nx, members * rows), BF16),
        scratch_shapes=[pltpu.VMEM((members * rows, bands * CAP), BF16), pltpu.VMEM((8, bands * CAP), F32)],
        compiler_params=params,
        name="zonal",
    )(length_x, got)
    turned = lax.all_to_all(zonal.reshape(bands, x_block, members * rows), "band", 0, 0, tiled=True)

    at = jnp.arange(bands * rows, dtype=jnp.int32)
    at_level, at_y = (at % rows) // ny_loc, at // rows * ny_loc + at % ny_loc
    to = jnp.arange(levels * ny, dtype=jnp.int32)
    to_level, to_y = to // ny, to % ny
    gap = jnp.abs(at_y[:, None] - to_y[None, :]).astype(F32)
    length = length_y[to_level][None, :]
    filter_y = jnp.where(
        at_level[:, None] == to_level[None, :], 2.0 / jnp.sqrt(length) * jnp.exp(-gap / length), 0.0
    ).astype(BF16)

    part = 8
    gradient, squares = pl.pallas_call(
        final_body,
        grid=(members // part,),
        in_specs=[
            pl.BlockSpec((bands, x_block, part * rows), lambda i: (0, 0, i)),
            pl.BlockSpec((bands * rows, levels * ny), lambda i: (0, 0)),
            pl.BlockSpec((part, levels, x_block, ny), lambda i: (i, 0, 0, 0)),
        ],
        out_specs=[
            pl.BlockSpec((part, levels, x_block, ny), lambda i: (i, 0, 0, 0)),
            pl.BlockSpec((8, ny), lambda i: (0, 0)),
        ],
        out_shape=[
            jax.ShapeDtypeStruct((members, levels, x_block, ny), F32),
            jax.ShapeDtypeStruct((8, ny), F32),
        ],
        scratch_shapes=[pltpu.VMEM((part * x_block, bands * rows), BF16)],
        compiler_params=params,
        name="final",
    )(turned, filter_y, control)

    partial_value = jnp.broadcast_to(jnp.sum(squares), (groups * bands, 1, 128))
    partials = lax.all_to_all(partial_value, ("mem", "band"), 0, 0, tiled=True)
    gradient_dot = jnp.sum(partials[:, 0, 0]) * (1.0 / (members * groups * levels * ny * nx))
    return (gradient, gradient_dot)


def solution(mesh):
    return jax.shard_map(
        on_device,
        mesh=mesh,
        in_specs=(
            P("mem", None, "band", None),
            P("mem", "band"),
            P("band"),
            P("band", None),
            P("band"),
            P(),
            P(),
        ),
        out_specs=(P("mem", None, "band", None), P()),
        check_vma=False,
    )
```

```python
import jax
import jax.numpy as jnp
from jax import lax
from jax.experimental import pallas as pl
from jax.experimental.pallas import tpu as pltpu
from jax.sharding import PartitionSpec as P

CAP = 128
HALF = 64
KEPT = 24
F32 = jnp.float32
BF16 = jnp.bfloat16
LOG2E = 1.4426950408889634
PARAMS = pltpu.CompilerParams(vmem_limit_bytes=56 * 1024 * 1024)
SMEM = pl.BlockSpec(memory_space=pltpu.SMEM)


def iota(shape, dim):
    return lax.broadcasted_iota(jnp.int32, shape, dim)


def flag(mask):
    return mask.astype(F32).astype(BF16)


def dot_last(a, b):
    return lax.dot_general(a, b, (((1,), (1,)), ((), ())), preferred_element_type=F32)


def rates(length):
    return LOG2E / length, 1.0 - (0.5 * LOG2E) * jnp.log(length)


def bucket_body(
    nx, rows, x_block, turn_ref, band_ref, cell_ref, weight_ref, pert_ref, out_ref, slot_ref, data_ref, masked_ref
):
    ends = out_ref.shape[0]
    members, obs = pert_ref.shape
    turn = turn_ref[0]
    earlier = flag(iota((128, 128), 0) < iota((128, 128), 1))
    cell = cell_ref[...]
    band = band_ref[...]
    row = ((cell.astype(F32) + 0.5) * (1.0 / nx)).astype(jnp.int32)
    col = cell - row * nx
    block = ((col.astype(F32) + 0.5) * (1.0 / x_block)).astype(jnp.int32)
    level = (row >= rows // 2).astype(jnp.int32)
    within = col - block * x_block
    data_ref[:members, :] = (weight_ref[...] * pert_ref[...].astype(F32)).astype(BF16)
    pick = iota((data_ref.shape[0] - members, obs), 0)
    coords = jnp.where(
        pick == 0, band, jnp.where(pick == 1, row, jnp.where(pick == 2, within, jnp.where(pick == 3, block, 0)))
    )
    data_ref[members:, :] = coords.astype(F32).astype(BF16)

    running = jnp.zeros((3 * ends, 1), F32)
    for part in range(obs // 128):
        at = slice(part * 128, (part + 1) * 128)
        key = iota((3 * ends, 128), 0)
        named = ((key == block[:, at] + ends * level[:, at]) | (key == band[:, at] + 2 * ends)).astype(F32)
        before = named * (jnp.dot(named.astype(BF16), earlier, preferred_element_type=F32) + running)
        rank = jnp.sum(before[: 2 * ends], axis=0, keepdims=True).astype(jnp.int32) - turn * HALF
        fits = (rank >= 0) & (rank < HALF)
        slot_ref[0:1, at] = jnp.where(fits, rank + HALF * level[:, at], -1)
        slot_ref[1:2, at] = jnp.sum(before[2 * ends :], axis=0, keepdims=True).astype(jnp.int32)
        running = running + jnp.sum(named, axis=1, keepdims=True)
    most = jnp.max(running[: 2 * ends], axis=0, keepdims=True).astype(jnp.int32)
    rounds = ((most + (HALF - 1)) >> 6).astype(F32)

    size = data_ref.shape[0]
    for side, dest in ((0, block), (1, band)):
        move = flag(iota((CAP, obs), 0) == slot_ref[side : side + 1, :])
        for end in range(ends):
            masked_ref[end * size : (end + 1) * size, :] = data_ref[...] * flag(dest == end)
        for end in range(0, ends, 8):
            packed = dot_last(masked_ref[end * size : (end + 8) * size, :], move).reshape(8, size, CAP)[:, :KEPT]
            if side == 0:
                packed = jnp.where(iota(packed.shape, 1) == members + 4, rounds[None], packed)
            out_ref[end : end + 8, :, side * CAP : (side + 1) * CAP] = packed.astype(BF16)


def states_body(rows, x_block, length_ref, got_ref, out_ref, a_ref, obs_ref):
    srcs = got_ref.shape[0]
    members = a_ref.shape[0] // rows
    for src in range(srcs):
        at = pl.ds(src * CAP, CAP)
        got = got_ref[src].astype(F32)
        row = got[members + 1 : members + 2]
        obs_ref[0:3, at] = got[members + 1 : members + 4]
        here = iota((rows, CAP), 0).astype(F32) == row
        for k in range(members):
            a_ref[k * rows : (k + 1) * rows, at] = jnp.where(here, got[k : k + 1], 0.0).astype(BF16)
    length = jnp.where(obs_ref[0:1, :] >= rows // 2, length_ref[1], length_ref[0])
    rate, scale = rates(length)
    within = obs_ref[1:2, :]
    place = iota((2 * srcs, srcs * CAP), 0)
    right = (place & 1) == 1
    ahead = (place >> 1) - obs_ref[2:3, :].astype(jnp.int32)
    steps = jnp.where(right, -ahead, ahead) & (srcs - 1)
    gap = (steps * x_block).astype(F32) + jnp.where(right, within - (x_block - 1.0), -within)
    apart = (steps >= 1) & (steps < srcs // 2)
    edge = jnp.where(apart, jnp.exp2(scale - jnp.maximum(gap, 0.0) * rate), 0.0).astype(BF16)
    value = dot_last(edge, a_ref[...]).astype(BF16)
    for block in range(srcs):
        out_ref[block] = value[2 * block : 2 * block + 2]


def decays(length, shape):
    rate = LOG2E / jnp.full(shape, length, F32)
    x = iota(shape, 0).astype(F32)
    return jnp.exp2(-x * rate), jnp.exp2((x - (shape[0] - 1.0)) * rate)


def near_body(
    ny_loc, nx, length_x_ref, length_y_ref, own_ref, far_ref, base_ref, out_ref, moments_ref, obs_ref, a_ref
):
    srcs = own_ref.shape[0]
    members, _, cols, ny = out_ref.shape
    level = pl.program_id(0)
    lanes = srcs * HALF
    first = iota((KEPT, CAP), 1) < HALF
    for which, ref in enumerate((own_ref, far_ref)):
        for src in range(0, srcs, 2):
            one, two = ref[src].astype(F32), ref[src + 1].astype(F32)
            low = jnp.where(first, one, pltpu.roll(two, HALF, 1))
            high = jnp.where(first, pltpu.roll(one, HALF, 1), two)
            at = which * lanes + src * HALF
            obs_ref[:, at : at + CAP] = jnp.where(level == 0, low, high)

    def constants(ref):
        return rates(jnp.full((1, CAP), ref[level], F32))

    def wide(value, shape):
        return jnp.broadcast_to(value[:, :1], shape)

    (rate_x, scale_x), (rate_y, scale_y) = constants(length_x_ref), constants(length_y_ref)
    chunk = 512
    total = jnp.zeros((members * cols, ny), F32)
    for part in range(2 * lanes // chunk):
        at = slice(part * chunk, (part + 1) * chunk)
        gap = jnp.abs(iota((cols, chunk), 0).astype(F32) - obs_ref[members + 2 : members + 3, at])
        if part * chunk >= lanes:
            gap = nx // 2 - gap
        filter_x = jnp.exp2(wide(scale_x, (1, chunk)) - gap * wide(rate_x, (1, chunk)))
        for k in range(members):
            a_ref[k * cols : (k + 1) * cols, at] = (filter_x * obs_ref[k : k + 1, at]).astype(BF16)
        row = obs_ref[members + 1 : members + 2, at] - (level * ny_loc).astype(F32)
        y = obs_ref[members : members + 1, at] * ny_loc + jnp.maximum(row, 0.0)
        gap = jnp.abs(iota((ny, chunk), 0).astype(F32) - y)
        filter_y = jnp.exp2(wide(scale_y, (1, chunk)) - gap * wide(rate_y, (1, chunk))).astype(BF16)
        total = total + dot_last(a_ref[:, at], filter_y)
    left, right = decays(length_x_ref[level], (cols, ny))
    for k in range(members):
        value = base_ref[k, 0].astype(F32) + total[k * cols : (k + 1) * cols]
        out_ref[k, 0] = value
        for which, factor in enumerate((left, right, value)):
            moments_ref[which, 0, k : k + 1] = jnp.sum(value * factor, axis=0, keepdims=True)


def edge_body(cols, length_x_ref, got_ref, fy_ref, moments_ref, out_ref, sum_ref, lhs_ref):
    bands, _, lanes = got_ref.shape
    _, levels, members, ny = out_ref.shape
    rows = lanes // members
    got = [got_ref[b].astype(F32) for b in range(bands)]
    for k in range(members):
        piece = jnp.concatenate([got[b][:, k * rows : (k + 1) * rows] for b in range(bands)], axis=1)
        lhs_ref[k : k + 1, :] = piece[0:1]
        lhs_ref[members + k : members + k + 1, :] = piece[1:2]
    edge = jnp.dot(lhs_ref[...].astype(BF16), fy_ref[...], preferred_element_type=F32)
    total = jnp.zeros((members, ny), F32)
    for level in range(levels):
        at = slice(level * ny, (level + 1) * ny)
        one, two = edge[:members, at], edge[members:, at]
        out_ref[0, level], out_ref[1, level] = one, two
        left, right = decays(length_x_ref[level], (cols, 128))

        def over_columns(value):
            return jnp.sum(value, axis=0, keepdims=True)[:, :1]

        total = total + moments_ref[2, level]
        total = total + one * (2.0 * moments_ref[0, level] + one * over_columns(left * left))
        total = total + two * (2.0 * moments_ref[1, level] + two * over_columns(right * right))
        total = total + one * two * (2.0 * over_columns(left * right))
    sum_ref[...] = jnp.full(sum_ref.shape, jnp.sum(total), F32)


def final_body(length_x_ref, edge_ref, near_ref, out_ref):
    part, levels, cols, ny = out_ref.shape
    for level in range(levels):
        left, right = decays(length_x_ref[level], (cols, ny))
        for k in range(part):
            one, two = edge_ref[0, level, k : k + 1], edge_ref[1, level, k : k + 1]
            out_ref[k, level] = near_ref[k, level] + left * one + right * two


def on_device(control, member_pert, obs_weight, obs_band, obs_cell, length_x, length_y):
    members, levels, x_block, ny = control.shape
    bands = lax.axis_size("band")
    groups = lax.axis_size("mem")
    ny_loc = ny // bands
    nx = x_block * bands
    obs = obs_cell.shape[0]
    rows = levels * ny_loc
    size = 32

    def route(turn, beside):
        packed = pl.pallas_call(
            lambda *refs: bucket_body(nx, rows, x_block, *refs),
            in_specs=[SMEM] + [pl.BlockSpec(memory_space=pltpu.VMEM)] * 4,
            out_shape=jax.ShapeDtypeStruct((bands, KEPT, 2 * CAP), BF16),
            scratch_shapes=[
                pltpu.VMEM((8, obs), jnp.int32),
                pltpu.VMEM((size, obs), BF16),
                pltpu.VMEM((bands * size, obs), BF16),
            ],
            compiler_params=PARAMS,
            name="bucket",
        )(turn, obs_band.reshape(1, obs), obs_cell.reshape(1, obs), obs_weight.reshape(1, obs), member_pert)
        got = lax.all_to_all(packed, "band", 0, 0, tiled=True)
        if beside is not None:
            got, beside = lax.optimization_barrier((got, beside))
        swap = [(i, (i + bands // 2) % bands) for i in range(bands)]
        return got, lax.ppermute(got[:, :, :CAP], "band", swap), beside

    def near_field(got, opposite, base):
        by_level = pl.BlockSpec((members, 1, x_block, ny), lambda i: (0, i, 0, 0))
        slots = 2 * bands * HALF
        return pl.pallas_call(
            lambda *refs: near_body(ny_loc, nx, *refs),
            grid=(levels,),
            in_specs=[
                SMEM,
                SMEM,
                pl.BlockSpec((bands, KEPT, CAP), lambda i: (0, 0, 0)),
                pl.BlockSpec((bands, KEPT, CAP), lambda i: (0, 0, 0)),
                by_level,
            ],
            out_specs=[by_level, pl.BlockSpec((3, 1, members, ny), lambda i: (0, i, 0, 0))],
            out_shape=[
                jax.ShapeDtypeStruct((members, levels, x_block, ny), F32),
                jax.ShapeDtypeStruct((3, levels, members, ny), F32),
            ],
            scratch_shapes=[pltpu.VMEM((KEPT, slots), F32), pltpu.VMEM((members * x_block, slots), BF16)],
            compiler_params=PARAMS,
            cost_estimate=pl.CostEstimate(
                flops=2 * levels * members * x_block * slots * ny, bytes_accessed=8_000_000, transcendentals=7_000_000
            ),
            name="near",
        )(length_x, length_y, got, opposite, base)

    at = jnp.arange(bands * rows, dtype=jnp.int32)
    at_level, at_y = (at % rows) // ny_loc, at // rows * ny_loc + at % ny_loc
    to = jnp.arange(levels * ny, dtype=jnp.int32)
    to_level, to_y = to // ny, to % ny
    gap = jnp.abs(at_y[:, None] - to_y[None, :]).astype(F32)
    length = length_y[to_level][None, :]
    filter_y = jnp.where(
        at_level[:, None] == to_level[None, :], 2.0 / jnp.sqrt(length) * jnp.exp(-gap / length), 0.0
    ).astype(BF16)

    got, opposite, filter_y = route(jnp.zeros((1,), jnp.int32), filter_y)
    states = pl.pallas_call(
        lambda *refs: states_body(rows, x_block, *refs),
        grid=(1,),
        in_specs=[SMEM, pl.BlockSpec((bands, KEPT, CAP), lambda i: (0, 0, 1))],
        out_specs=pl.BlockSpec((bands, 2, members * rows), lambda i: (0, 0, 0)),
        out_shape=jax.ShapeDtypeStruct((bands, 2, members * rows), BF16),
        scratch_shapes=[pltpu.VMEM((members * rows, bands * CAP), BF16), pltpu.VMEM((8, bands * CAP), F32)],
        compiler_params=PARAMS,
        name="states",
    )(length_x, got)
    edges = lax.all_to_all(states, "band", 0, 0, tiled=True)

    near, moments = near_field(got, opposite, control)
    rounds = jnp.max(got[:, members + 4, 0].astype(F32)).astype(jnp.int32)

    def again(carry):
        turn, near, _ = carry
        more, more_opposite, _ = route(turn.reshape(1), None)
        return (turn + 1, *near_field(more, more_opposite, near))

    _, near, moments = lax.while_loop(lambda carry: carry[0] < rounds, again, (jnp.int32(1), near, moments))

    edge, partial_value = pl.pallas_call(
        lambda *refs: edge_body(x_block, *refs),
        in_specs=[SMEM] + [pl.BlockSpec(memory_space=pltpu.VMEM)] * 3,
        out_shape=[
            jax.ShapeDtypeStruct((2, levels, members, ny), F32),
            jax.ShapeDtypeStruct((groups * bands, 128), F32),
        ],
        scratch_shapes=[pltpu.VMEM((2 * members, bands * rows), F32)],
        compiler_params=PARAMS,
        name="edge",
    )(length_x, edges, filter_y, moments)
    partials = lax.all_to_all(partial_value, ("mem", "band"), 0, 0, tiled=True)

    part = 8
    by_member = pl.BlockSpec((part, levels, x_block, ny), lambda i: (i, 0, 0, 0))
    gradient = pl.pallas_call(
        final_body,
        grid=(members // part,),
        in_specs=[SMEM, pl.BlockSpec((2, levels, part, ny), lambda i: (0, 0, i, 0)), by_member],
        out_specs=by_member,
        out_shape=jax.ShapeDtypeStruct((members, levels, x_block, ny), F32),
        compiler_params=PARAMS,
        cost_estimate=pl.CostEstimate(flops=20_000_000, bytes_accessed=10_000_000, transcendentals=0),
        name="final",
    )(length_x, edge, near)
    gradient_dot = jnp.sum(partials[:, 0]) * (1.0 / (members * groups * levels * ny * nx))
    return (gradient, gradient_dot)


def solution(mesh):
    return jax.shard_map(
        on_device,
        mesh=mesh,
        in_specs=(
            P("mem", None, "band", None),
            P("mem", "band"),
            P("band"),
            P("band", None),
            P("band"),
            P(),
            P(),
        ),
        out_specs=(P("mem", None, "band", None), P()),
        check_vma=False,
    )
```

```python
import jax
import jax.numpy as jnp
from jax import lax
from jax.experimental import pallas as pl
from jax.experimental.pallas import tpu as pltpu
from jax.sharding import PartitionSpec as P

CAP = 128
HALF = 64
KEPT = 24
F32 = jnp.float32
BF16 = jnp.bfloat16
LOG2E = 1.4426950408889634
SMEM = pl.BlockSpec(memory_space=pltpu.SMEM)


def iota(shape, dim):
    return lax.broadcasted_iota(jnp.int32, shape, dim)


def room(mib):
    return pltpu.CompilerParams(vmem_limit_bytes=mib * 1024 * 1024)


def flag(mask):
    return mask.astype(F32).astype(BF16)


def dot_last(a, b):
    return lax.dot_general(a, b, (((1,), (1,)), ((), ())), preferred_element_type=F32)


def rates(length):
    return LOG2E / length, 1.0 - (0.5 * LOG2E) * jnp.log(length)


def bucket_body(
    nx, rows, x_block, turn_ref, band_ref, cell_ref, weight_ref, pert_ref, out_ref, slot_ref, data_ref, masked_ref
):
    ends = out_ref.shape[0]
    members, obs = pert_ref.shape
    turn = turn_ref[0]
    earlier = flag(iota((128, 128), 0) < iota((128, 128), 1))
    cell = cell_ref[...]
    band = band_ref[...]
    row = ((cell.astype(F32) + 0.5) * (1.0 / nx)).astype(jnp.int32)
    col = cell - row * nx
    block = ((col.astype(F32) + 0.5) * (1.0 / x_block)).astype(jnp.int32)
    level = (row >= rows // 2).astype(jnp.int32)
    within = col - block * x_block
    data_ref[:members, :] = (weight_ref[...] * pert_ref[...].astype(F32)).astype(BF16)
    pick = iota((data_ref.shape[0] - members, obs), 0)
    coords = jnp.zeros(pick.shape, jnp.int32)
    for at, value in ((0, band), (1, row), (2, within), (4, row), (5, within), (6, block)):
        coords = jnp.where(pick == at, value, coords)
    data_ref[members:, :] = coords.astype(F32).astype(BF16)

    running = jnp.zeros((3 * ends, 1), F32)
    for part in range(obs // 128):
        at = slice(part * 128, (part + 1) * 128)
        key = iota((3 * ends, 128), 0)
        named = ((key == block[:, at] + ends * level[:, at]) | (key == band[:, at] + 2 * ends)).astype(F32)
        before = named * (jnp.dot(named.astype(BF16), earlier, preferred_element_type=F32) + running)
        rank = jnp.sum(before[: 2 * ends], axis=0, keepdims=True).astype(jnp.int32) - turn * HALF
        fits = (rank >= 0) & (rank < HALF)
        slot_ref[0:1, at] = jnp.where(fits, rank + HALF * level[:, at], -1)
        slot_ref[1:2, at] = jnp.sum(before[2 * ends :], axis=0, keepdims=True).astype(jnp.int32)
        running = running + jnp.sum(named, axis=1, keepdims=True)
    counts = running[: 2 * ends].astype(jnp.int32)
    rounds = ((jnp.max(counts, axis=0, keepdims=True) + (HALF - 1)) >> 6).astype(F32)
    filled = jnp.clip(counts - turn * HALF, 0, HALF).astype(F32)

    size = data_ref.shape[0]
    place = iota((KEPT - members, CAP), 0)
    half = iota((1, CAP), 1) < HALF
    for side, dest in ((0, block), (1, band)):
        move = flag(iota((CAP, obs), 0) == slot_ref[side : side + 1, :])
        for end in range(ends):
            masked_ref[end * size : (end + 1) * size, :] = data_ref[...] * flag(dest == end)
        for first in range(0, ends, 8):
            packed = dot_last(masked_ref[first * size : (first + 8) * size, :], move)
            for end in range(first, first + 8):
                own = packed[(end - first) * size : (end - first + 1) * size]
                found = own[members:KEPT]
                if side == 0:
                    out_ref[end, :members, :] = own[:members].astype(BF16)
                    both = jnp.where(half, filled[end : end + 1], filled[ends + end : ends + end + 1])
                    found = jnp.where(place == 3, rounds, jnp.where(place == 7, both, found))
                    out_ref[end, members:KEPT, :] = found.astype(BF16)
                else:
                    out_ref[end, KEPT:, :] = own[:members].astype(BF16)
                    kept = out_ref[end, members:KEPT, :].astype(F32)
                    theirs = (place >= 4) & (place < 7)
                    out_ref[end, members:KEPT, :] = jnp.where(theirs, found, kept).astype(BF16)


def states_body(rows, x_block, length_ref, got_ref, out_ref, a_ref, obs_ref):
    srcs = got_ref.shape[0]
    members = a_ref.shape[0] // rows
    for src in range(srcs):
        at = pl.ds(src * CAP, CAP)
        got = got_ref[src].astype(F32)
        row = got[members + 4 : members + 5]
        obs_ref[0:3, at] = got[members + 4 : members + 7]
        here = iota((rows, CAP), 0).astype(F32) == row
        for k in range(members):
            payload = got[KEPT + k : KEPT + k + 1]
            a_ref[k * rows : (k + 1) * rows, at] = jnp.where(here, payload, 0.0).astype(BF16)
    length = jnp.where(obs_ref[0:1, :] >= rows // 2, length_ref[1], length_ref[0])
    rate, scale = rates(length)
    within = obs_ref[1:2, :]
    place = iota((2 * srcs, srcs * CAP), 0)
    right = (place & 1) == 1
    ahead = (place >> 1) - obs_ref[2:3, :].astype(jnp.int32)
    steps = jnp.where(right, -ahead, ahead) & (srcs - 1)
    gap = (steps * x_block).astype(F32) + jnp.where(right, within - (x_block - 1.0), -within)
    apart = (steps >= 1) & (steps < srcs // 2)
    edge = jnp.where(apart, jnp.exp2(scale - jnp.maximum(gap, 0.0) * rate), 0.0).astype(BF16)
    value = dot_last(edge, a_ref[...]).astype(BF16)
    for block in range(srcs):
        out_ref[block] = value[2 * block : 2 * block + 2]


def decays(length, shape):
    rate = LOG2E / jnp.full(shape, length, F32)
    x = iota(shape, 0).astype(F32)
    return jnp.exp2(-x * rate), jnp.exp2((x - (shape[0] - 1.0)) * rate)


def filter_body(rows, length_ref, out_ref):
    some, ny = out_ref.shape
    at = iota((some, 128), 0) + pl.program_id(0) * some
    band = ((at.astype(F32) + 0.5) * (1.0 / rows)).astype(jnp.int32)
    row = at - band * rows
    level = (row >= rows // 2).astype(jnp.int32)
    y = (band * (rows // 2) + row - level * (rows // 2)).astype(F32)[:, :1]
    rate, scale = rates(jnp.where(level == 1, length_ref[1], length_ref[0]))
    gap = jnp.abs(iota((some, ny), 1).astype(F32) - y)
    out_ref[...] = jnp.exp2(scale[:, :1] - gap * rate[:, :1]).astype(BF16)


def near_body(
    ny_loc,
    nx,
    length_x_ref,
    length_y_ref,
    own_ref,
    far_ref,
    base_ref,
    out_ref,
    moments_ref,
    rounds_ref,
    obs_ref,
    total_ref,
    count_ref,
    scalar_ref,
    *buffers,
):
    srcs = own_ref.shape[0]
    members, _, cols, ny = out_ref.shape
    level = pl.program_id(0)
    lane = iota((KEPT, CAP), 1)
    last = iota((KEPT, CAP), 0) == KEPT - 1

    @pl.when(level == 0)
    def _():
        most = jnp.zeros((8, CAP), F32)
        for which, ref in enumerate((own_ref, far_ref)):
            for src in range(srcs):
                coords = ref[src, members:KEPT, :].astype(F32)
                at = which * srcs + src
                count_ref[at : at + 1, :] = coords[7:8].astype(jnp.int32)
                most = jnp.maximum(most, coords)
        rounds_ref[0] = jnp.max(jnp.where(iota((8, CAP), 0) == 3, most, 0.0)).astype(jnp.int32)
        pltpu.sync_copy(count_ref, scalar_ref)

    filled = jnp.int32(0)
    now = jnp.zeros((KEPT, CAP), F32)
    for which, ref in enumerate((own_ref, far_ref)):
        for src in range(srcs):
            count = scalar_ref[which * srcs + src, level * HALF]
            start = filled & (CAP - 1)
            value = jnp.where(last, float(which), ref[src].astype(F32))
            value = pltpu.roll(value, (start - level * HALF) & (CAP - 1), 1)
            valid = ((lane - start) & (CAP - 1)) < count
            now = jnp.where(valid & (lane >= start), value, now)
            obs_ref[filled >> 7] = now
            now = jnp.where(start + count >= CAP, jnp.where(valid & (lane < start), value, 0.0), now)
            filled = filled + count
    obs_ref[filled >> 7] = now
    for more in range(1, 7):
        obs_ref[(filled >> 7) + more] = jnp.zeros((KEPT, CAP), F32)

    def constants(ref, shape):
        rate, scale = rates(jnp.full((8, CAP), ref[level], F32))
        return jnp.broadcast_to(rate[:1], shape), jnp.broadcast_to(scale[:1], shape)

    rate_x, scale_x = constants(length_x_ref, (1, CAP))
    rate_y, scale_y = constants(length_y_ref, (1, CAP))
    step = 2 * CAP

    def build(which, a_ref, fy_ref):
        for piece in range(2):
            at = slice(piece * CAP, (piece + 1) * CAP)
            slots = obs_ref[2 * which + piece]
            opposite = slots[KEPT - 1 : KEPT]
            gap = jnp.abs(iota((cols, CAP), 0).astype(F32) - slots[members + 2 : members + 3])
            gap = opposite * (nx // 2) + (1.0 - 2.0 * opposite) * gap
            filter_x = jnp.exp2(scale_x - gap * rate_x)
            for k in range(members):
                a_ref[k * cols : (k + 1) * cols, at] = (filter_x * slots[k : k + 1]).astype(BF16)
            row = slots[members + 1 : members + 2] - (level * ny_loc).astype(F32)
            y = slots[members : members + 1] * ny_loc + jnp.maximum(row, 0.0)
            gap = jnp.abs(iota((ny, CAP), 0).astype(F32) - y)
            fy_ref[:, at] = jnp.exp2(scale_y - gap * rate_y).astype(BF16)

    one, two = buffers[:2], buffers[2:]
    total_ref[...] = jnp.zeros(total_ref.shape, F32)
    build(0, *one)

    def pair(i, carry):
        build(2 * i + 1, *two)
        total_ref[...] = total_ref[...] + dot_last(one[0][...], one[1][...])
        build(2 * i + 2, *one)
        total_ref[...] = total_ref[...] + dot_last(two[0][...], two[1][...])
        return carry

    lax.fori_loop(0, (filled + (2 * step - 1)) >> 9, pair, 0)

    left, right = decays(length_x_ref[level], (cols, ny))
    for k in range(members):
        value = base_ref[k, 0].astype(F32) + total_ref[k * cols : (k + 1) * cols, :]
        out_ref[k, 0] = value
        for which, factor in enumerate((left, right, value)):
            moments_ref[which, 0, k : k + 1] = jnp.sum(value * factor, axis=0, keepdims=True)


def edge_body(cols, length_x_ref, got_ref, fy_ref, level_ref, moments_ref, out_ref, sum_ref, lhs_ref):
    bands, _, lanes = got_ref.shape
    _, levels, members, ny = out_ref.shape
    rows = lanes // members
    got = [got_ref[b].astype(F32) for b in range(bands)]
    for k in range(members):
        piece = jnp.concatenate([got[b][:, k * rows : (k + 1) * rows] for b in range(bands)], axis=1)
        lhs_ref[k : k + 1, :] = piece[0:1]
        lhs_ref[members + k : members + k + 1, :] = piece[1:2]
    lhs = lhs_ref[...]
    level_of = level_ref[0:1, :]
    lhs = jnp.concatenate([jnp.where(level_of == level, lhs, 0.0).astype(BF16) for level in range(levels)], axis=0)
    edge = jnp.dot(lhs, fy_ref[...], preferred_element_type=F32)
    total = jnp.zeros((members, ny), F32)
    for level in range(levels):
        at = 2 * level * members
        one, two = edge[at : at + members], edge[at + members : at + 2 * members]
        out_ref[0, level], out_ref[1, level] = one, two
        left, right = decays(length_x_ref[level], (cols, 128))

        def over_columns(value):
            return jnp.sum(value, axis=0, keepdims=True)[:, :1]

        total = total + moments_ref[2, level]
        total = total + one * (2.0 * moments_ref[0, level] + one * over_columns(left * left))
        total = total + two * (2.0 * moments_ref[1, level] + two * over_columns(right * right))
        total = total + one * two * (2.0 * over_columns(left * right))
    sum_ref[...] = jnp.full(sum_ref.shape, jnp.sum(total), F32)


def final_body(length_x_ref, edge_ref, near_ref, out_ref):
    part, levels, cols, ny = out_ref.shape
    for level in range(levels):
        left, right = decays(length_x_ref[level], (cols, ny))
        for k in range(part):
            one, two = edge_ref[0, level, k : k + 1], edge_ref[1, level, k : k + 1]
            out_ref[k, level] = near_ref[k, level] + left * one + right * two


def on_device(control, member_pert, obs_weight, obs_band, obs_cell, length_x, length_y):
    members, levels, x_block, ny = control.shape
    bands = lax.axis_size("band")
    groups = lax.axis_size("mem")
    ny_loc = ny // bands
    nx = x_block * bands
    obs = obs_cell.shape[0]
    rows = levels * ny_loc
    size = 32

    def route(turn, beside=None):
        packed = pl.pallas_call(
            lambda *refs: bucket_body(nx, rows, x_block, *refs),
            in_specs=[SMEM] + [pl.BlockSpec(memory_space=pltpu.VMEM)] * 4,
            out_shape=jax.ShapeDtypeStruct((bands, KEPT + members, CAP), BF16),
            scratch_shapes=[
                pltpu.VMEM((8, obs), jnp.int32),
                pltpu.VMEM((size, obs), BF16),
                pltpu.VMEM((bands * size, obs), BF16),
            ],
            compiler_params=room(16),
            name="bucket",
        )(turn, obs_band.reshape(1, obs), obs_cell.reshape(1, obs), obs_weight.reshape(1, obs), member_pert)
        got = lax.all_to_all(packed, "band", 0, 0, tiled=True)
        if beside is not None:
            got, beside = lax.optimization_barrier((got, beside))
        own = got[:, :KEPT]
        swap = [(i, (i + bands // 2) % bands) for i in range(bands)]
        return got, own, lax.ppermute(own, "band", swap), beside

    def near_field(own, opposite, base):
        by_level = pl.BlockSpec((members, 1, x_block, ny), lambda i: (0, i, 0, 0))
        slots = 2 * bands * HALF
        buffers = [pltpu.VMEM((members * x_block, 2 * CAP), BF16), pltpu.VMEM((ny, 2 * CAP), BF16)]
        return pl.pallas_call(
            lambda *refs: near_body(ny_loc, nx, *refs),
            grid=(levels,),
            in_specs=[
                SMEM,
                SMEM,
                pl.BlockSpec((bands, KEPT, CAP), lambda i: (0, 0, 0)),
                pl.BlockSpec((bands, KEPT, CAP), lambda i: (0, 0, 0)),
                by_level,
            ],
            out_specs=[by_level, pl.BlockSpec((3, 1, members, ny), lambda i: (0, i, 0, 0)), SMEM],
            out_shape=[
                jax.ShapeDtypeStruct((members, levels, x_block, ny), F32),
                jax.ShapeDtypeStruct((3, levels, members, ny), F32),
                jax.ShapeDtypeStruct((1,), jnp.int32),
            ],
            scratch_shapes=[
                pltpu.VMEM((slots // CAP + 8, KEPT, CAP), F32),
                pltpu.VMEM((members * x_block, ny), F32),
                pltpu.VMEM((2 * bands, CAP), jnp.int32),
                pltpu.SMEM((2 * bands, CAP), jnp.int32),
                *buffers,
                *buffers,
            ],
            compiler_params=room(28),
            cost_estimate=pl.CostEstimate(
                flops=levels * members * x_block * slots * ny, bytes_accessed=8_000_000, transcendentals=4_000_000
            ),
            name="near",
        )(length_x, length_y, own, opposite, base)

    some = 8 * rows
    filter_y = pl.pallas_call(
        lambda *refs: filter_body(rows, *refs),
        grid=(bands * rows // some,),
        in_specs=[SMEM],
        out_specs=pl.BlockSpec((some, ny), lambda i: (i, 0)),
        out_shape=jax.ShapeDtypeStruct((bands * rows, ny), BF16),
        compiler_params=room(16),
        cost_estimate=pl.CostEstimate(flops=5_000_000, bytes_accessed=3_000_000, transcendentals=1_200_000),
        name="filter",
    )(length_y)

    got, own, opposite, filter_y = route(jnp.zeros((1,), jnp.int32), filter_y)
    states = pl.pallas_call(
        lambda *refs: states_body(rows, x_block, *refs),
        in_specs=[SMEM, pl.BlockSpec(memory_space=pltpu.VMEM)],
        out_shape=jax.ShapeDtypeStruct((bands, 2, members * rows), BF16),
        scratch_shapes=[pltpu.VMEM((members * rows, bands * CAP), BF16), pltpu.VMEM((8, bands * CAP), F32)],
        compiler_params=room(20),
        name="states",
    )(length_x, got)
    edges = lax.all_to_all(states, "band", 0, 0, tiled=True)

    near, moments, rounds = near_field(own, opposite, control)

    def again(carry):
        turn, near, _ = carry
        _, more, more_opposite, _ = route(turn.reshape(1))
        return (turn + 1, *near_field(more, more_opposite, near)[:2])

    _, near, moments = lax.while_loop(lambda carry: carry[0] < rounds[0], again, (jnp.int32(1), near, moments))

    level_of = jnp.broadcast_to(jnp.arange(bands * rows, dtype=jnp.int32) // ny_loc % levels, (8, bands * rows))
    edge, partial_value = pl.pallas_call(
        lambda *refs: edge_body(x_block, *refs),
        in_specs=[SMEM] + [pl.BlockSpec(memory_space=pltpu.VMEM)] * 4,
        out_shape=[
            jax.ShapeDtypeStruct((2, levels, members, ny), F32),
            jax.ShapeDtypeStruct((groups * bands, 128), F32),
        ],
        scratch_shapes=[pltpu.VMEM((2 * members, bands * rows), F32)],
        compiler_params=room(16),
        name="edge",
    )(length_x, edges, filter_y, level_of, moments)
    partials = lax.all_to_all(partial_value, ("mem", "band"), 0, 0, tiled=True)

    part = 8
    by_member = pl.BlockSpec((part, levels, x_block, ny), lambda i: (i, 0, 0, 0))
    gradient = pl.pallas_call(
        final_body,
        grid=(members // part,),
        in_specs=[SMEM, pl.BlockSpec((2, levels, part, ny), lambda i: (0, 0, i, 0)), by_member],
        out_specs=by_member,
        out_shape=jax.ShapeDtypeStruct((members, levels, x_block, ny), F32),
        compiler_params=room(24),
        cost_estimate=pl.CostEstimate(flops=20_000_000, bytes_accessed=10_000_000, transcendentals=0),
        name="final",
    )(length_x, edge, near)
    gradient_dot = jnp.sum(partials[:, 0]) * (1.0 / (members * groups * levels * ny * nx))
    return (gradient, gradient_dot)


def solution(mesh):
    return jax.shard_map(
        on_device,
        mesh=mesh,
        in_specs=(
            P("mem", None, "band", None),
            P("mem", "band"),
            P("band"),
            P("band", None),
            P("band"),
            P(),
            P(),
        ),
        out_specs=(P("mem", None, "band", None), P()),
        check_vma=False,
    )
```

```python
import jax
import jax.numpy as jnp
from jax import lax
from jax.experimental import pallas as pl
from jax.experimental.pallas import tpu as pltpu
from jax.sharding import PartitionSpec as P

CAP = 128
HALF = 64
KEPT = 24
USUAL = 2304
WIDE = 256
F32 = jnp.float32
BF16 = jnp.bfloat16
LOG2E = 1.4426950408889634
SMEM = pl.BlockSpec(memory_space=pltpu.SMEM)


def iota(shape, dim):
    return lax.broadcasted_iota(jnp.int32, shape, dim)


def room(mib):
    return pltpu.CompilerParams(vmem_limit_bytes=mib * 1024 * 1024)


def flag(mask):
    return mask.astype(F32).astype(BF16)


def dot_last(a, b):
    return lax.dot_general(a, b, (((1,), (1,)), ((), ())), preferred_element_type=F32)


def rates(length):
    return LOG2E / length, 1.0 - (0.5 * LOG2E) * jnp.log(length)


def bucket_body(
    nx, rows, x_block, turn_ref, band_ref, cell_ref, weight_ref, pert_ref, out_ref, slot_ref, data_ref, masked_ref
):
    ends = out_ref.shape[0]
    members, obs = pert_ref.shape
    turn = turn_ref[0]
    earlier = flag(iota((128, 128), 0) < iota((128, 128), 1))
    cell = cell_ref[...]
    band = band_ref[...]
    row = ((cell.astype(F32) + 0.5) * (1.0 / nx)).astype(jnp.int32)
    col = cell - row * nx
    block = ((col.astype(F32) + 0.5) * (1.0 / x_block)).astype(jnp.int32)
    level = (row >= rows // 2).astype(jnp.int32)
    within = col - block * x_block
    data_ref[:members, :] = (weight_ref[...] * pert_ref[...].astype(F32)).astype(BF16)
    pick = iota((data_ref.shape[0] - members, obs), 0)
    coords = jnp.zeros(pick.shape, jnp.int32)
    for at, value in ((0, band), (1, row), (2, within), (4, row), (5, within), (6, block)):
        coords = jnp.where(pick == at, value, coords)
    data_ref[members:, :] = coords.astype(F32).astype(BF16)

    running = jnp.zeros((3 * ends, 1), F32)
    for part in range(obs // 128):
        at = slice(part * 128, (part + 1) * 128)
        key = iota((3 * ends, 128), 0)
        named = ((key == block[:, at] + ends * level[:, at]) | (key == band[:, at] + 2 * ends)).astype(F32)
        before = named * (jnp.dot(named.astype(BF16), earlier, preferred_element_type=F32) + running)
        rank = jnp.sum(before[: 2 * ends], axis=0, keepdims=True).astype(jnp.int32) - turn * HALF
        fits = (rank >= 0) & (rank < HALF)
        slot_ref[0:1, at] = jnp.where(fits, rank + HALF * level[:, at], -1)
        slot_ref[1:2, at] = jnp.sum(before[2 * ends :], axis=0, keepdims=True).astype(jnp.int32)
        running = running + jnp.sum(named, axis=1, keepdims=True)
    counts = running[: 2 * ends].astype(jnp.int32)
    rounds = ((jnp.max(counts, axis=0, keepdims=True) + (HALF - 1)) >> 6).astype(F32)
    filled = jnp.clip(counts - turn * HALF, 0, HALF).astype(F32)

    size = data_ref.shape[0]
    place = iota((KEPT - members, CAP), 0)
    half = iota((1, CAP), 1) < HALF
    for side, dest in ((0, block), (1, band)):
        move = flag(iota((CAP, obs), 0) == slot_ref[side : side + 1, :])
        for end in range(ends):
            masked_ref[end * size : (end + 1) * size, :] = data_ref[...] * flag(dest == end)
        for first in range(0, ends, 8):
            packed = dot_last(masked_ref[first * size : (first + 8) * size, :], move)
            for end in range(first, first + 8):
                own = packed[(end - first) * size : (end - first + 1) * size]
                found = own[members:KEPT]
                if side == 0:
                    out_ref[end, :members, :] = own[:members].astype(BF16)
                    both = jnp.where(half, filled[end : end + 1], filled[ends + end : ends + end + 1])
                    found = jnp.where(place == 3, rounds, jnp.where(place == 7, both, found))
                    out_ref[end, members:KEPT, :] = found.astype(BF16)
                else:
                    out_ref[end, KEPT:, :] = own[:members].astype(BF16)
                    kept = out_ref[end, members:KEPT, :].astype(F32)
                    theirs = (place >= 4) & (place < 7)
                    out_ref[end, members:KEPT, :] = jnp.where(theirs, found, kept).astype(BF16)


def states_body(rows, x_block, length_ref, got_ref, out_ref, a_ref, obs_ref):
    srcs = got_ref.shape[0]
    members = a_ref.shape[0] // rows
    for src in range(srcs):
        at = pl.ds(src * CAP, CAP)
        got = got_ref[src].astype(F32)
        row = got[members + 4 : members + 5]
        obs_ref[0:3, at] = got[members + 4 : members + 7]
        here = iota((rows, CAP), 0).astype(F32) == row
        for k in range(members):
            payload = got[KEPT + k : KEPT + k + 1]
            a_ref[k * rows : (k + 1) * rows, at] = jnp.where(here, payload, 0.0).astype(BF16)
    length = jnp.where(obs_ref[0:1, :] >= rows // 2, length_ref[1], length_ref[0])
    rate, scale = rates(length)
    within = obs_ref[1:2, :]
    place = iota((2 * srcs, srcs * CAP), 0)
    right = (place & 1) == 1
    ahead = (place >> 1) - obs_ref[2:3, :].astype(jnp.int32)
    steps = jnp.where(right, -ahead, ahead) & (srcs - 1)
    gap = (steps * x_block).astype(F32) + jnp.where(right, within - (x_block - 1.0), -within)
    apart = (steps >= 1) & (steps < srcs // 2)
    edge = jnp.where(apart, jnp.exp2(scale - jnp.maximum(gap, 0.0) * rate), 0.0).astype(BF16)
    value = dot_last(edge, a_ref[...]).astype(BF16)
    for block in range(srcs):
        out_ref[block] = value[2 * block : 2 * block + 2]


def decays(length, shape):
    rate = LOG2E / jnp.full(shape, length, F32)
    x = iota(shape, 0).astype(F32)
    return jnp.exp2(-x * rate), jnp.exp2((x - (shape[0] - 1.0)) * rate)


def filter_body(rows, length_ref, out_ref):
    some, ny = out_ref.shape
    at = iota((some, 128), 0) + pl.program_id(0) * some
    band = ((at.astype(F32) + 0.5) * (1.0 / rows)).astype(jnp.int32)
    row = at - band * rows
    level = (row >= rows // 2).astype(jnp.int32)
    y = (band * (rows // 2) + row - level * (rows // 2)).astype(F32)[:, :1]
    rate, scale = rates(jnp.where(level == 1, length_ref[1], length_ref[0]))
    gap = jnp.abs(iota((some, ny), 1).astype(F32) - y)
    out_ref[...] = jnp.exp2(scale[:, :1] - gap * rate[:, :1]).astype(BF16)


def near_body(
    ny_loc,
    nx,
    length_x_ref,
    length_y_ref,
    own_ref,
    far_ref,
    base_ref,
    out_ref,
    moments_ref,
    rounds_ref,
    obs_ref,
    total_ref,
    count_ref,
    scalar_ref,
    a_ref,
):
    srcs = own_ref.shape[0]
    members, _, cols, ny = out_ref.shape
    level = pl.program_id(0)
    lane = iota((KEPT, CAP), 1)
    last = iota((KEPT, CAP), 0) == KEPT - 1

    @pl.when(level == 0)
    def _():
        most = counts = jnp.zeros((8, CAP), F32)
        for which, ref in enumerate((own_ref, far_ref)):
            for src in range(srcs):
                coords = ref[src, members:KEPT, :].astype(F32)
                here = (iota((8, CAP), 1) & (HALF - 1)) == which * srcs + src
                counts = jnp.where(here, coords, counts)
                most = jnp.maximum(most, coords)
        rounds_ref[0] = jnp.max(jnp.where(iota((8, CAP), 0) == 3, most, 0.0)).astype(jnp.int32)
        count_ref[0:1, :] = counts[7:8].astype(jnp.int32)
        pltpu.sync_copy(count_ref, scalar_ref)

    for block in range(USUAL // CAP):
        obs_ref[block] = jnp.zeros((KEPT, CAP), F32)
    filled = jnp.int32(0)
    now = jnp.zeros((KEPT, CAP), F32)
    for which, ref in enumerate((own_ref, far_ref)):
        for src in range(srcs):
            count = scalar_ref[0, level * HALF + which * srcs + src]
            start = filled & (CAP - 1)
            value = jnp.where(last, float(which), ref[src].astype(F32))
            value = pltpu.roll(value, (start - level * HALF) & (CAP - 1), 1)
            valid = ((lane - start) & (CAP - 1)) < count
            now = jnp.where(valid & (lane >= start), value, now)
            obs_ref[filled >> 7] = now
            now = jnp.where(start + count >= CAP, jnp.where(valid & (lane < start), value, 0.0), now)
            filled = filled + count
    obs_ref[filled >> 7] = now
    obs_ref[(filled >> 7) + 1] = jnp.zeros((KEPT, CAP), F32)

    def constants(ref, shape):
        rate, scale = rates(jnp.full((8, CAP), ref[level], F32))
        return jnp.broadcast_to(rate[:1], shape), jnp.broadcast_to(scale[:1], shape)

    rate_x, scale_x = constants(length_x_ref, (1, CAP))
    rate_y, scale_y = constants(length_y_ref, (1, CAP))
    def build(at, blocks):
        pieces = []
        for piece, slots in enumerate(blocks):
            lanes = slice(at + piece * CAP, at + (piece + 1) * CAP)
            opposite = slots[KEPT - 1 : KEPT]
            gap = jnp.abs(iota((cols, CAP), 0).astype(F32) - slots[members + 2 : members + 3])
            gap = opposite * (nx // 2) + (1.0 - 2.0 * opposite) * gap
            filter_x = jnp.exp2(scale_x - gap * rate_x)
            for k in range(members):
                a_ref[k * cols : (k + 1) * cols, lanes] = (filter_x * slots[k : k + 1]).astype(BF16)
            row = slots[members + 1 : members + 2] - (level * ny_loc).astype(F32)
            y = slots[members : members + 1] * ny_loc + jnp.maximum(row, 0.0)
            gap = jnp.abs(iota((ny, CAP), 0).astype(F32) - y)
            pieces.append(jnp.exp2(scale_y - gap * rate_y).astype(BF16))
        size = len(blocks) * CAP
        return dot_last(a_ref[:, at : at + size], jnp.concatenate(pieces, axis=1))

    total = jnp.zeros(total_ref.shape, F32)
    for at in range(0, USUAL, WIDE):
        some = range(at // CAP, min(at + WIDE, USUAL) // CAP)
        total = total + build(at, [obs_ref[block] for block in some])
    total_ref[...] = total

    def more(i, carry):
        total_ref[...] = total_ref[...] + build(0, [obs_ref[2 * i], obs_ref[2 * i + 1]])
        return carry

    lax.fori_loop(USUAL // (2 * CAP), (filled + (2 * CAP - 1)) >> 8, more, 0)

    left, right = decays(length_x_ref[level], (cols, ny))
    for k in range(members):
        value = base_ref[k, 0].astype(F32) + total_ref[k * cols : (k + 1) * cols, :]
        out_ref[k, 0] = value
        for which, factor in enumerate((left, right, value)):
            moments_ref[which, 0, k : k + 1] = jnp.sum(value * factor, axis=0, keepdims=True)


def edge_body(cols, length_x_ref, got_ref, fy_ref, level_ref, moments_ref, out_ref, sum_ref, lhs_ref):
    bands, _, lanes = got_ref.shape
    _, levels, members, ny = out_ref.shape
    rows = lanes // members
    got = [got_ref[b].astype(F32) for b in range(bands)]
    for k in range(members):
        piece = jnp.concatenate([got[b][:, k * rows : (k + 1) * rows] for b in range(bands)], axis=1)
        lhs_ref[k : k + 1, :] = piece[0:1]
        lhs_ref[members + k : members + k + 1, :] = piece[1:2]
    lhs = lhs_ref[...]
    level_of = level_ref[0:1, :]
    lhs = jnp.concatenate([jnp.where(level_of == level, lhs, 0.0).astype(BF16) for level in range(levels)], axis=0)
    edge = jnp.dot(lhs, fy_ref[...], preferred_element_type=F32)
    total = jnp.zeros((members, ny), F32)
    for level in range(levels):
        at = 2 * level * members
        one, two = edge[at : at + members], edge[at + members : at + 2 * members]
        out_ref[0, level], out_ref[1, level] = one, two
        left, right = decays(length_x_ref[level], (cols, 128))

        def over_columns(value):
            return jnp.sum(value, axis=0, keepdims=True)[:, :1]

        total = total + moments_ref[2, level]
        total = total + one * (2.0 * moments_ref[0, level] + one * over_columns(left * left))
        total = total + two * (2.0 * moments_ref[1, level] + two * over_columns(right * right))
        total = total + one * two * (2.0 * over_columns(left * right))
    sum_ref[...] = jnp.full(sum_ref.shape, jnp.sum(total), F32)


def final_body(length_x_ref, edge_ref, near_ref, out_ref):
    part, levels, cols, ny = out_ref.shape
    for level in range(levels):
        left, right = decays(length_x_ref[level], (cols, ny))
        for k in range(part):
            one, two = edge_ref[0, level, k : k + 1], edge_ref[1, level, k : k + 1]
            out_ref[k, level] = near_ref[k, level] + left * one + right * two


def on_device(control, member_pert, obs_weight, obs_band, obs_cell, length_x, length_y):
    members, levels, x_block, ny = control.shape
    bands = lax.axis_size("band")
    groups = lax.axis_size("mem")
    ny_loc = ny // bands
    nx = x_block * bands
    obs = obs_cell.shape[0]
    rows = levels * ny_loc
    size = 32

    def route(turn, beside=None):
        packed = pl.pallas_call(
            lambda *refs: bucket_body(nx, rows, x_block, *refs),
            in_specs=[SMEM] + [pl.BlockSpec(memory_space=pltpu.VMEM)] * 4,
            out_shape=jax.ShapeDtypeStruct((bands, KEPT + members, CAP), BF16),
            scratch_shapes=[
                pltpu.VMEM((8, obs), jnp.int32),
                pltpu.VMEM((size, obs), BF16),
                pltpu.VMEM((bands * size, obs), BF16),
            ],
            compiler_params=room(16),
            name="bucket",
        )(turn, obs_band.reshape(1, obs), obs_cell.reshape(1, obs), obs_weight.reshape(1, obs), member_pert)
        got = lax.all_to_all(packed, "band", 0, 0, tiled=True)
        if beside is not None:
            got, beside = lax.optimization_barrier((got, beside))
        own = got[:, :KEPT]
        swap = [(i, (i + bands // 2) % bands) for i in range(bands)]
        return got, own, lax.ppermute(own, "band", swap), beside

    def near_field(own, opposite, base):
        by_level = pl.BlockSpec((members, 1, x_block, ny), lambda i: (0, i, 0, 0))
        slots = 2 * bands * HALF
        return pl.pallas_call(
            lambda *refs: near_body(ny_loc, nx, *refs),
            grid=(levels,),
            in_specs=[
                SMEM,
                SMEM,
                pl.BlockSpec((bands, KEPT, CAP), lambda i: (0, 0, 0)),
                pl.BlockSpec((bands, KEPT, CAP), lambda i: (0, 0, 0)),
                by_level,
            ],
            out_specs=[by_level, pl.BlockSpec((3, 1, members, ny), lambda i: (0, i, 0, 0)), SMEM],
            out_shape=[
                jax.ShapeDtypeStruct((members, levels, x_block, ny), F32),
                jax.ShapeDtypeStruct((3, levels, members, ny), F32),
                jax.ShapeDtypeStruct((1,), jnp.int32),
            ],
            scratch_shapes=[
                pltpu.VMEM((slots // CAP + 8, KEPT, CAP), F32),
                pltpu.VMEM((members * x_block, ny), F32),
                pltpu.VMEM((1, CAP), jnp.int32),
                pltpu.SMEM((1, CAP), jnp.int32),
                pltpu.VMEM((members * x_block, USUAL), BF16),
            ],
            compiler_params=room(52),
            cost_estimate=pl.CostEstimate(
                flops=levels * members * x_block * slots * ny, bytes_accessed=8_000_000, transcendentals=4_000_000
            ),
            name="near",
        )(length_x, length_y, own, opposite, base)

    some = 8 * rows
    filter_y = pl.pallas_call(
        lambda *refs: filter_body(rows, *refs),
        grid=(bands * rows // some,),
        in_specs=[SMEM],
        out_specs=pl.BlockSpec((some, ny), lambda i: (i, 0)),
        out_shape=jax.ShapeDtypeStruct((bands * rows, ny), BF16),
        compiler_params=room(16),
        cost_estimate=pl.CostEstimate(flops=5_000_000, bytes_accessed=3_000_000, transcendentals=1_200_000),
        name="filter",
    )(length_y)

    got, own, opposite, filter_y = route(jnp.zeros((1,), jnp.int32), filter_y)
    states = pl.pallas_call(
        lambda *refs: states_body(rows, x_block, *refs),
        in_specs=[SMEM, pl.BlockSpec(memory_space=pltpu.VMEM)],
        out_shape=jax.ShapeDtypeStruct((bands, 2, members * rows), BF16),
        scratch_shapes=[pltpu.VMEM((members * rows, bands * CAP), BF16), pltpu.VMEM((8, bands * CAP), F32)],
        compiler_params=room(20),
        name="states",
    )(length_x, got)
    edges = lax.all_to_all(states, "band", 0, 0, tiled=True)

    near, moments, rounds = near_field(own, opposite, control)

    def again(carry):
        turn, near, _ = carry
        _, more, more_opposite, _ = route(turn.reshape(1))
        return (turn + 1, *near_field(more, more_opposite, near)[:2])

    _, near, moments = lax.while_loop(lambda carry: carry[0] < rounds[0], again, (jnp.int32(1), near, moments))

    level_of = jnp.broadcast_to(jnp.arange(bands * rows, dtype=jnp.int32) // ny_loc % levels, (8, bands * rows))
    edge, partial_value = pl.pallas_call(
        lambda *refs: edge_body(x_block, *refs),
        in_specs=[SMEM] + [pl.BlockSpec(memory_space=pltpu.VMEM)] * 4,
        out_shape=[
            jax.ShapeDtypeStruct((2, levels, members, ny), F32),
            jax.ShapeDtypeStruct((groups * bands, 128), F32),
        ],
        scratch_shapes=[pltpu.VMEM((2 * members, bands * rows), F32)],
        compiler_params=room(16),
        name="edge",
    )(length_x, edges, filter_y, level_of, moments)
    partials = lax.all_to_all(partial_value, ("mem", "band"), 0, 0, tiled=True)

    part = 8
    by_member = pl.BlockSpec((part, levels, x_block, ny), lambda i: (i, 0, 0, 0))
    gradient = pl.pallas_call(
        final_body,
        grid=(members // part,),
        in_specs=[SMEM, pl.BlockSpec((2, levels, part, ny), lambda i: (0, 0, i, 0)), by_member],
        out_specs=by_member,
        out_shape=jax.ShapeDtypeStruct((members, levels, x_block, ny), F32),
        compiler_params=room(24),
        cost_estimate=pl.CostEstimate(flops=20_000_000, bytes_accessed=10_000_000, transcendentals=0),
        name="final",
    )(length_x, edge, near)
    gradient_dot = jnp.sum(partials[:, 0]) * (1.0 / (members * groups * levels * ny * nx))
    return (gradient, gradient_dot)


def solution(mesh):
    return jax.shard_map(
        on_device,
        mesh=mesh,
        in_specs=(
            P("mem", None, "band", None),
            P("mem", "band"),
            P("band"),
            P("band", None),
            P("band"),
            P(),
            P(),
        ),
        out_specs=(P("mem", None, "band", None), P()),
        check_vma=False,
    )
```

```python
import jax
import jax.numpy as jnp
from jax import lax
from jax.experimental import pallas as pl
from jax.experimental.pallas import tpu as pltpu
from jax.sharding import PartitionSpec as P

CAP = 128
HALF = 64
KEPT = 24
USUAL = 2304
WIDE = 256
F32 = jnp.float32
BF16 = jnp.bfloat16
LOG2E = 1.4426950408889634
SMEM = pl.BlockSpec(memory_space=pltpu.SMEM)


def iota(shape, dim):
    return lax.broadcasted_iota(jnp.int32, shape, dim)


def room(mib):
    return pltpu.CompilerParams(vmem_limit_bytes=mib * 1024 * 1024)


def flag(mask):
    return mask.astype(F32).astype(BF16)


def dot_last(a, b):
    return lax.dot_general(a, b, (((1,), (1,)), ((), ())), preferred_element_type=F32)


def rates(length):
    return LOG2E / length, 1.0 - (0.5 * LOG2E) * jnp.log(length)


def bucket_body(
    nx, rows, x_block, turn_ref, band_ref, cell_ref, weight_ref, pert_ref, out_ref, slot_ref, data_ref, masked_ref
):
    ends = out_ref.shape[0]
    members, obs = pert_ref.shape
    turn = turn_ref[0]
    earlier = flag(iota((128, 128), 0) < iota((128, 128), 1))
    cell = cell_ref[...]
    band = band_ref[...]
    row = ((cell.astype(F32) + 0.5) * (1.0 / nx)).astype(jnp.int32)
    col = cell - row * nx
    block = ((col.astype(F32) + 0.5) * (1.0 / x_block)).astype(jnp.int32)
    level = (row >= rows // 2).astype(jnp.int32)
    within = col - block * x_block
    data_ref[:members, :] = (weight_ref[...] * pert_ref[...].astype(F32)).astype(BF16)
    pick = iota((data_ref.shape[0] - members, obs), 0) & (KEPT - members - 1)
    coords = jnp.zeros(pick.shape, jnp.int32)
    for at, value in ((0, band), (1, row), (2, within), (4, row), (5, within), (6, block)):
        coords = jnp.where(pick == at, value, coords)
    data_ref[members:, :] = coords.astype(F32).astype(BF16)

    running = jnp.zeros((3 * ends, 1), F32)
    for part in range(obs // 128):
        at = slice(part * 128, (part + 1) * 128)
        key = iota((3 * ends, 128), 0)
        named = ((key == block[:, at] + ends * level[:, at]) | (key == band[:, at] + 2 * ends)).astype(F32)
        before = named * (jnp.dot(named.astype(BF16), earlier, preferred_element_type=F32) + running)
        rank = jnp.sum(before[: 2 * ends], axis=0, keepdims=True).astype(jnp.int32) - turn * HALF
        fits = (rank >= 0) & (rank < HALF)
        slot_ref[0:1, at] = jnp.where(fits, rank + HALF * level[:, at], -1)
        slot_ref[1:2, at] = jnp.sum(before[2 * ends :], axis=0, keepdims=True).astype(jnp.int32)
        running = running + jnp.sum(named, axis=1, keepdims=True)
    counts = running[: 2 * ends].astype(jnp.int32)
    rounds = ((jnp.max(counts, axis=0, keepdims=True) + (HALF - 1)) >> 6).astype(F32)
    filled = jnp.clip(counts - turn * HALF, 0, HALF).astype(F32)

    extra = KEPT - members
    size = 2 * KEPT
    place = iota((extra, CAP), 0)
    half = iota((1, CAP), 1) < HALF
    upper = iota((2 * extra, obs), 0) < extra
    for side, dest in ((0, block), (1, band)):
        move = flag(iota((CAP, obs), 0) == slot_ref[side : side + 1, :])
        for end in range(0, ends, 2):
            at = end // 2 * size
            one, two = flag(dest == end), flag(dest == end + 1)
            masked_ref[at : at + members, :] = data_ref[:members, :] * one
            masked_ref[at + members : at + 2 * members, :] = data_ref[:members, :] * two
            either = flag(dest == jnp.where(upper, end, end + 1))
            masked_ref[at + 2 * members : at + size, :] = data_ref[members:, :] * either
        for first in range(0, ends, 8):
            packed = dot_last(masked_ref[first // 2 * size : (first // 2 + 4) * size, :], move)
            for end in range(first, first + 8):
                at = (end - first) // 2 * size
                own = packed[at + end % 2 * members : at + end % 2 * members + members]
                at = at + 2 * members + end % 2 * extra
                found = packed[at : at + extra]
                if side == 0:
                    out_ref[end, :members, :] = own.astype(BF16)
                    both = jnp.where(half, filled[end : end + 1], filled[ends + end : ends + end + 1])
                    found = jnp.where(place == 3, rounds, jnp.where(place == 7, both, found))
                    out_ref[end, members:KEPT, :] = found.astype(BF16)
                else:
                    out_ref[end, KEPT:, :] = own.astype(BF16)
                    kept = out_ref[end, members:KEPT, :].astype(F32)
                    theirs = (place >= 4) & (place < 7)
                    out_ref[end, members:KEPT, :] = jnp.where(theirs, found, kept).astype(BF16)


def states_body(rows, x_block, length_ref, got_ref, out_ref, a_ref, obs_ref):
    srcs = got_ref.shape[0]
    members = a_ref.shape[0] // rows
    group = 4
    value = jnp.zeros((2 * srcs, members * rows), F32)
    for first in range(0, srcs, group):
        lanes = slice(first * CAP, (first + group) * CAP)
        for src in range(first, first + group):
            at = slice(src * CAP, (src + 1) * CAP)
            got = got_ref[src].astype(F32)
            row = got[members + 4 : members + 5]
            obs_ref[0:3, at] = got[members + 4 : members + 7]
            here = iota((rows, CAP), 0).astype(F32) == row
            for k in range(members):
                payload = got[KEPT + k : KEPT + k + 1]
                a_ref[k * rows : (k + 1) * rows, at] = jnp.where(here, payload, 0.0).astype(BF16)
        length = jnp.where(obs_ref[0:1, lanes] >= rows // 2, length_ref[1], length_ref[0])
        rate, scale = rates(length)
        within = obs_ref[1:2, lanes]
        place = iota((2 * srcs, group * CAP), 0)
        right = (place & 1) == 1
        ahead = (place >> 1) - obs_ref[2:3, lanes].astype(jnp.int32)
        steps = jnp.where(right, -ahead, ahead) & (srcs - 1)
        gap = (steps * x_block).astype(F32) + jnp.where(right, within - (x_block - 1.0), -within)
        apart = (steps >= 1) & (steps < srcs // 2)
        edge = jnp.where(apart, jnp.exp2(scale - jnp.maximum(gap, 0.0) * rate), 0.0).astype(BF16)
        value = value + dot_last(edge, a_ref[:, lanes])
    value = value.astype(BF16)
    for block in range(srcs):
        out_ref[block] = value[2 * block : 2 * block + 2]


def decays(length, shape):
    rate = LOG2E / jnp.full(shape, length, F32)
    x = iota(shape, 0).astype(F32)
    return jnp.exp2(-x * rate), jnp.exp2((x - (shape[0] - 1.0)) * rate)


def filter_body(rows, length_ref, out_ref):
    some, ny = out_ref.shape
    at = iota((some, 128), 0) + pl.program_id(0) * some
    band = ((at.astype(F32) + 0.5) * (1.0 / rows)).astype(jnp.int32)
    row = at - band * rows
    level = (row >= rows // 2).astype(jnp.int32)
    y = (band * (rows // 2) + row - level * (rows // 2)).astype(F32)[:, :1]
    rate, scale = rates(jnp.where(level == 1, length_ref[1], length_ref[0]))
    gap = jnp.abs(iota((some, ny), 1).astype(F32) - y)
    out_ref[...] = jnp.exp2(scale[:, :1] - gap * rate[:, :1]).astype(BF16)


def near_body(
    ny_loc,
    nx,
    length_x_ref,
    length_y_ref,
    own_ref,
    far_ref,
    base_ref,
    out_ref,
    moments_ref,
    rounds_ref,
    obs_ref,
    total_ref,
    count_ref,
    scalar_ref,
    a_ref,
):
    srcs = own_ref.shape[0]
    members, _, cols, ny = out_ref.shape
    level = pl.program_id(0)
    lane = iota((KEPT, CAP), 1)
    last = iota((KEPT, CAP), 0) == KEPT - 1

    @pl.when(level == 0)
    def _():
        most = counts = jnp.zeros((8, CAP), F32)
        for which, ref in enumerate((own_ref, far_ref)):
            for src in range(srcs):
                coords = ref[src, members:KEPT, :].astype(F32)
                here = (iota((8, CAP), 1) & (HALF - 1)) == which * srcs + src
                counts = jnp.where(here, coords, counts)
                most = jnp.maximum(most, coords)
        rounds_ref[0] = jnp.max(jnp.where(iota((8, CAP), 0) == 3, most, 0.0)).astype(jnp.int32)
        count_ref[0:1, :] = counts[7:8].astype(jnp.int32)
        pltpu.sync_copy(count_ref, scalar_ref)

    for block in range(USUAL // CAP):
        obs_ref[block] = jnp.zeros((KEPT, CAP), F32)
    filled = jnp.int32(0)
    now = jnp.zeros((KEPT, CAP), F32)
    for which, ref in enumerate((own_ref, far_ref)):
        for src in range(srcs):
            count = scalar_ref[0, level * HALF + which * srcs + src]
            start = filled & (CAP - 1)
            value = jnp.where(last, float(which), ref[src].astype(F32))
            value = pltpu.roll(value, (start - level * HALF) & (CAP - 1), 1)
            valid = ((lane - start) & (CAP - 1)) < count
            now = jnp.where(valid & (lane >= start), value, now)
            obs_ref[filled >> 7] = now
            now = jnp.where(start + count >= CAP, jnp.where(valid & (lane < start), value, 0.0), now)
            filled = filled + count
    obs_ref[filled >> 7] = now
    obs_ref[(filled >> 7) + 1] = jnp.zeros((KEPT, CAP), F32)

    def constants(ref, shape):
        rate, scale = rates(jnp.full((8, CAP), ref[level], F32))
        return jnp.broadcast_to(rate[:1], shape), jnp.broadcast_to(scale[:1], shape)

    rate_x, scale_x = constants(length_x_ref, (1, CAP))
    rate_y, scale_y = constants(length_y_ref, (1, CAP))
    def build(at, blocks):
        pieces = []
        for piece, slots in enumerate(blocks):
            lanes = slice(at + piece * CAP, at + (piece + 1) * CAP)
            opposite = slots[KEPT - 1 : KEPT]
            gap = jnp.abs(iota((cols, CAP), 0).astype(F32) - slots[members + 2 : members + 3])
            gap = opposite * (nx // 2) + (1.0 - 2.0 * opposite) * gap
            filter_x = jnp.exp2(scale_x - gap * rate_x)
            for k in range(members):
                a_ref[k * cols : (k + 1) * cols, lanes] = (filter_x * slots[k : k + 1]).astype(BF16)
            row = slots[members + 1 : members + 2] - (level * ny_loc).astype(F32)
            y = slots[members : members + 1] * ny_loc + jnp.maximum(row, 0.0)
            gap = jnp.abs(iota((ny, CAP), 0).astype(F32) - y)
            pieces.append(jnp.exp2(scale_y - gap * rate_y).astype(BF16))
        size = len(blocks) * CAP
        return dot_last(a_ref[:, at : at + size], jnp.concatenate(pieces, axis=1))

    total = jnp.zeros(total_ref.shape, F32)
    for at in range(0, USUAL, WIDE):
        some = range(at // CAP, min(at + WIDE, USUAL) // CAP)
        total = total + build(at, [obs_ref[block] for block in some])
    total_ref[...] = total

    def more(i, carry):
        total_ref[...] = total_ref[...] + build(0, [obs_ref[2 * i], obs_ref[2 * i + 1]])
        return carry

    lax.fori_loop(USUAL // (2 * CAP), (filled + (2 * CAP - 1)) >> 8, more, 0)

    left, right = decays(length_x_ref[level], (cols, ny))
    for k in range(members):
        value = base_ref[k, 0].astype(F32) + total_ref[k * cols : (k + 1) * cols, :]
        out_ref[k, 0] = value
        for which, factor in enumerate((left, right, value)):
            moments_ref[which, 0, k : k + 1] = jnp.sum(value * factor, axis=0, keepdims=True)


def edge_body(cols, length_x_ref, got_ref, fy_ref, level_ref, moments_ref, out_ref, sum_ref, lhs_ref):
    bands, _, lanes = got_ref.shape
    _, levels, members, ny = out_ref.shape
    rows = lanes // members
    got = [got_ref[b].astype(F32) for b in range(bands)]
    for k in range(members):
        piece = jnp.concatenate([got[b][:, k * rows : (k + 1) * rows] for b in range(bands)], axis=1)
        lhs_ref[k : k + 1, :] = piece[0:1]
        lhs_ref[members + k : members + k + 1, :] = piece[1:2]
    lhs = lhs_ref[...]
    level_of = level_ref[0:1, :]
    lhs = jnp.concatenate([jnp.where(level_of == level, lhs, 0.0).astype(BF16) for level in range(levels)], axis=0)
    edge = jnp.dot(lhs, fy_ref[...], preferred_element_type=F32)
    total = jnp.zeros((members, ny), F32)
    for level in range(levels):
        at = 2 * level * members
        one, two = edge[at : at + members], edge[at + members : at + 2 * members]
        out_ref[0, level], out_ref[1, level] = one, two
        left, right = decays(length_x_ref[level], (cols, 128))

        def over_columns(value):
            return jnp.sum(value, axis=0, keepdims=True)[:, :1]

        total = total + moments_ref[2, level]
        total = total + one * (2.0 * moments_ref[0, level] + one * over_columns(left * left))
        total = total + two * (2.0 * moments_ref[1, level] + two * over_columns(right * right))
        total = total + one * two * (2.0 * over_columns(left * right))
    sum_ref[...] = jnp.full(sum_ref.shape, jnp.sum(total), F32)


def final_body(length_x_ref, edge_ref, near_ref, out_ref):
    part, levels, cols, ny = out_ref.shape
    for level in range(levels):
        left, right = decays(length_x_ref[level], (cols, ny))
        for k in range(part):
            one, two = edge_ref[0, level, k : k + 1], edge_ref[1, level, k : k + 1]
            out_ref[k, level] = near_ref[k, level] + left * one + right * two


def on_device(control, member_pert, obs_weight, obs_band, obs_cell, length_x, length_y):
    members, levels, x_block, ny = control.shape
    bands = lax.axis_size("band")
    groups = lax.axis_size("mem")
    ny_loc = ny // bands
    nx = x_block * bands
    obs = obs_cell.shape[0]
    rows = levels * ny_loc
    size = 2 * (KEPT - members)

    def route(turn, beside=None):
        packed = pl.pallas_call(
            lambda *refs: bucket_body(nx, rows, x_block, *refs),
            in_specs=[SMEM] + [pl.BlockSpec(memory_space=pltpu.VMEM)] * 4,
            out_shape=jax.ShapeDtypeStruct((bands, KEPT + members, CAP), BF16),
            scratch_shapes=[
                pltpu.VMEM((8, obs), jnp.int32),
                pltpu.VMEM((members + size, obs), BF16),
                pltpu.VMEM((bands * KEPT, obs), BF16),
            ],
            compiler_params=room(16),
            name="bucket",
        )(turn, obs_band.reshape(1, obs), obs_cell.reshape(1, obs), obs_weight.reshape(1, obs), member_pert)
        got = lax.all_to_all(packed, "band", 0, 0, tiled=True)
        if beside is not None:
            got, beside = lax.optimization_barrier((got, beside))
        own = got[:, :KEPT]
        swap = [(i, (i + bands // 2) % bands) for i in range(bands)]
        return got, own, lax.ppermute(own, "band", swap), beside

    def near_field(own, opposite, base):
        by_level = pl.BlockSpec((members, 1, x_block, ny), lambda i: (0, i, 0, 0))
        slots = 2 * bands * HALF
        return pl.pallas_call(
            lambda *refs: near_body(ny_loc, nx, *refs),
            grid=(levels,),
            in_specs=[
                SMEM,
                SMEM,
                pl.BlockSpec((bands, KEPT, CAP), lambda i: (0, 0, 0)),
                pl.BlockSpec((bands, KEPT, CAP), lambda i: (0, 0, 0)),
                by_level,
            ],
            out_specs=[by_level, pl.BlockSpec((3, 1, members, ny), lambda i: (0, i, 0, 0)), SMEM],
            out_shape=[
                jax.ShapeDtypeStruct((members, levels, x_block, ny), F32),
                jax.ShapeDtypeStruct((3, levels, members, ny), F32),
                jax.ShapeDtypeStruct((1,), jnp.int32),
            ],
            scratch_shapes=[
                pltpu.VMEM((slots // CAP + 8, KEPT, CAP), F32),
                pltpu.VMEM((members * x_block, ny), F32),
                pltpu.VMEM((1, CAP), jnp.int32),
                pltpu.SMEM((1, CAP), jnp.int32),
                pltpu.VMEM((members * x_block, USUAL), BF16),
            ],
            compiler_params=room(52),
            cost_estimate=pl.CostEstimate(
                flops=levels * members * x_block * slots * ny, bytes_accessed=8_000_000, transcendentals=4_000_000
            ),
            name="near",
        )(length_x, length_y, own, opposite, base)

    some = 8 * rows
    filter_y = pl.pallas_call(
        lambda *refs: filter_body(rows, *refs),
        grid=(bands * rows // some,),
        in_specs=[SMEM],
        out_specs=pl.BlockSpec((some, ny), lambda i: (i, 0)),
        out_shape=jax.ShapeDtypeStruct((bands * rows, ny), BF16),
        compiler_params=room(16),
        cost_estimate=pl.CostEstimate(flops=5_000_000, bytes_accessed=3_000_000, transcendentals=1_200_000),
        name="filter",
    )(length_y)

    got, own, opposite, filter_y = route(jnp.zeros((1,), jnp.int32), filter_y)
    states = pl.pallas_call(
        lambda *refs: states_body(rows, x_block, *refs),
        in_specs=[SMEM, pl.BlockSpec(memory_space=pltpu.VMEM)],
        out_shape=jax.ShapeDtypeStruct((bands, 2, members * rows), BF16),
        scratch_shapes=[pltpu.VMEM((members * rows, bands * CAP), BF16), pltpu.VMEM((8, bands * CAP), F32)],
        compiler_params=room(20),
        name="states",
    )(length_x, got)
    edges = lax.all_to_all(states, "band", 0, 0, tiled=True)

    near, moments, rounds = near_field(own, opposite, control)

    def again(carry):
        turn, near, _ = carry
        _, more, more_opposite, _ = route(turn.reshape(1))
        return (turn + 1, *near_field(more, more_opposite, near)[:2])

    _, near, moments = lax.while_loop(lambda carry: carry[0] < rounds[0], again, (jnp.int32(1), near, moments))

    level_of = jnp.broadcast_to(jnp.arange(bands * rows, dtype=jnp.int32) // ny_loc % levels, (8, bands * rows))
    edge, partial_value = pl.pallas_call(
        lambda *refs: edge_body(x_block, *refs),
        in_specs=[SMEM] + [pl.BlockSpec(memory_space=pltpu.VMEM)] * 4,
        out_shape=[
            jax.ShapeDtypeStruct((2, levels, members, ny), F32),
            jax.ShapeDtypeStruct((groups * bands, 128), F32),
        ],
        scratch_shapes=[pltpu.VMEM((2 * members, bands * rows), F32)],
        compiler_params=room(16),
        name="edge",
    )(length_x, edges, filter_y, level_of, moments)
    partials = lax.all_to_all(partial_value, ("mem", "band"), 0, 0, tiled=True)

    part = 8
    by_member = pl.BlockSpec((part, levels, x_block, ny), lambda i: (i, 0, 0, 0))
    gradient = pl.pallas_call(
        final_body,
        grid=(members // part,),
        in_specs=[SMEM, pl.BlockSpec((2, levels, part, ny), lambda i: (0, 0, i, 0)), by_member],
        out_specs=by_member,
        out_shape=jax.ShapeDtypeStruct((members, levels, x_block, ny), F32),
        compiler_params=room(24),
        cost_estimate=pl.CostEstimate(flops=20_000_000, bytes_accessed=10_000_000, transcendentals=0),
        name="final",
    )(length_x, edge, near)
    gradient_dot = jnp.sum(partials[:, 0]) * (1.0 / (members * groups * levels * ny * nx))
    return (gradient, gradient_dot)


def solution(mesh):
    return jax.shard_map(
        on_device,
        mesh=mesh,
        in_specs=(
            P("mem", None, "band", None),
            P("mem", "band"),
            P("band"),
            P("band", None),
            P("band"),
            P(),
            P(),
        ),
        out_specs=(P("mem", None, "band", None), P()),
        check_vma=False,
    )
```

```python
import jax
import jax.numpy as jnp
from jax import lax
from jax.experimental import pallas as pl
from jax.experimental.pallas import tpu as pltpu
from jax.sharding import PartitionSpec as P

CAP = 128
HALF = 64
KEPT = 24
USUAL = 2304
WIDE = 256
F32 = jnp.float32
BF16 = jnp.bfloat16
LOG2E = 1.4426950408889634
SMEM = pl.BlockSpec(memory_space=pltpu.SMEM)


def iota(shape, dim):
    return lax.broadcasted_iota(jnp.int32, shape, dim)


def room(mib):
    return pltpu.CompilerParams(vmem_limit_bytes=mib * 1024 * 1024)


def flag(mask):
    return mask.astype(F32).astype(BF16)


def dot_last(a, b):
    return lax.dot_general(a, b, (((1,), (1,)), ((), ())), preferred_element_type=F32)


def rates(length):
    return LOG2E / length, 1.0 - (0.5 * LOG2E) * jnp.log(length)


def bucket_body(
    nx, rows, x_block, turn_ref, band_ref, cell_ref, weight_ref, pert_ref, out_ref, slot_ref, data_ref, masked_ref
):
    ends = out_ref.shape[0]
    members, obs = pert_ref.shape
    turn = turn_ref[0]
    earlier = flag(iota((128, 128), 0) < iota((128, 128), 1))
    cell = cell_ref[...]
    band = band_ref[...]
    row = ((cell.astype(F32) + 0.5) * (1.0 / nx)).astype(jnp.int32)
    col = cell - row * nx
    block = ((col.astype(F32) + 0.5) * (1.0 / x_block)).astype(jnp.int32)
    level = (row >= rows // 2).astype(jnp.int32)
    within = col - block * x_block
    data_ref[:members, :] = (weight_ref[...] * pert_ref[...].astype(F32)).astype(BF16)
    pick = iota((data_ref.shape[0] - members, obs), 0) & (KEPT - members - 1)
    coords = jnp.zeros(pick.shape, jnp.int32)
    for at, value in ((0, band), (1, row), (2, within), (4, row), (5, within), (6, block)):
        coords = jnp.where(pick == at, value, coords)
    data_ref[members:, :] = coords.astype(F32).astype(BF16)

    running = jnp.zeros((3 * ends, 1), F32)
    for part in range(obs // 128):
        at = slice(part * 128, (part + 1) * 128)
        key = iota((3 * ends, 128), 0)
        named = ((key == block[:, at] + ends * level[:, at]) | (key == band[:, at] + 2 * ends)).astype(F32)
        before = named * (jnp.dot(named.astype(BF16), earlier, preferred_element_type=F32) + running)
        rank = jnp.sum(before[: 2 * ends], axis=0, keepdims=True).astype(jnp.int32) - turn * HALF
        fits = (rank >= 0) & (rank < HALF)
        slot_ref[0:1, at] = jnp.where(fits, rank + HALF * level[:, at], -1)
        slot_ref[1:2, at] = jnp.sum(before[2 * ends :], axis=0, keepdims=True).astype(jnp.int32)
        running = running + jnp.sum(named, axis=1, keepdims=True)
    counts = running[: 2 * ends].astype(jnp.int32)
    rounds = ((jnp.max(counts, axis=0, keepdims=True) + (HALF - 1)) >> 6).astype(F32)
    filled = jnp.clip(counts - turn * HALF, 0, HALF).astype(F32)

    extra = KEPT - members
    size = 2 * KEPT
    place = iota((extra, CAP), 0)
    half = iota((1, CAP), 1) < HALF
    upper = iota((2 * extra, obs), 0) < extra
    for side, dest in ((0, block), (1, band)):
        move = flag(iota((CAP, obs), 0) == slot_ref[side : side + 1, :])
        for end in range(0, ends, 2):
            at = end // 2 * size
            one, two = flag(dest == end), flag(dest == end + 1)
            masked_ref[at : at + members, :] = data_ref[:members, :] * one
            masked_ref[at + members : at + 2 * members, :] = data_ref[:members, :] * two
            either = flag(dest == jnp.where(upper, end, end + 1))
            masked_ref[at + 2 * members : at + size, :] = data_ref[members:, :] * either
        for first in range(0, ends, 8):
            packed = dot_last(masked_ref[first // 2 * size : (first // 2 + 4) * size, :], move)
            for end in range(first, first + 8):
                at = (end - first) // 2 * size
                own = packed[at + end % 2 * members : at + end % 2 * members + members]
                at = at + 2 * members + end % 2 * extra
                found = packed[at : at + extra]
                if side == 0:
                    out_ref[end, :members, :] = own.astype(BF16)
                    both = jnp.where(half, filled[end : end + 1], filled[ends + end : ends + end + 1])
                    found = jnp.where(place == 3, rounds, jnp.where(place == 7, both, found))
                    out_ref[end, members:KEPT, :] = found.astype(BF16)
                else:
                    out_ref[end, KEPT:, :] = own.astype(BF16)
                    kept = out_ref[end, members:KEPT, :].astype(F32)
                    theirs = (place >= 4) & (place < 7)
                    out_ref[end, members:KEPT, :] = jnp.where(theirs, found, kept).astype(BF16)


def states_body(rows, x_block, length_ref, got_ref, out_ref, a_ref, obs_ref):
    srcs = got_ref.shape[0]
    members = a_ref.shape[0] // rows
    group = 4
    value = jnp.zeros((2 * srcs, members * rows), F32)
    for first in range(0, srcs, group):
        lanes = slice(first * CAP, (first + group) * CAP)
        for src in range(first, first + group):
            at = slice(src * CAP, (src + 1) * CAP)
            got = got_ref[src].astype(F32)
            row = got[members + 4 : members + 5]
            obs_ref[0:3, at] = got[members + 4 : members + 7]
            here = iota((rows, CAP), 0).astype(F32) == row
            for k in range(members):
                payload = got[KEPT + k : KEPT + k + 1]
                a_ref[k * rows : (k + 1) * rows, at] = jnp.where(here, payload, 0.0).astype(BF16)
        length = jnp.where(obs_ref[0:1, lanes] >= rows // 2, length_ref[1], length_ref[0])
        rate, scale = rates(length)
        within = obs_ref[1:2, lanes]
        place = iota((2 * srcs, group * CAP), 0)
        right = (place & 1) == 1
        ahead = (place >> 1) - obs_ref[2:3, lanes].astype(jnp.int32)
        steps = jnp.where(right, -ahead, ahead) & (srcs - 1)
        gap = (steps * x_block).astype(F32) + jnp.where(right, within - (x_block - 1.0), -within)
        apart = (steps >= 1) & (steps < srcs // 2)
        edge = jnp.where(apart, jnp.exp2(scale - jnp.maximum(gap, 0.0) * rate), 0.0).astype(BF16)
        value = value + dot_last(edge, a_ref[:, lanes])
    value = value.astype(BF16)
    for block in range(srcs):
        out_ref[block] = value[2 * block : 2 * block + 2]


def decays(length, shape):
    rate = LOG2E / jnp.full(shape, length, F32)
    x = iota(shape, 0).astype(F32)
    return jnp.exp2(-x * rate), jnp.exp2((x - (shape[0] - 1.0)) * rate)


def filter_body(rows, length_ref, out_ref):
    some, ny = out_ref.shape
    at = iota((some, 128), 0) + pl.program_id(0) * some
    band = ((at.astype(F32) + 0.5) * (1.0 / rows)).astype(jnp.int32)
    row = at - band * rows
    level = (row >= rows // 2).astype(jnp.int32)
    y = (band * (rows // 2) + row - level * (rows // 2)).astype(F32)[:, :1]
    rate, scale = rates(jnp.where(level == 1, length_ref[1], length_ref[0]))
    gap = jnp.abs(iota((some, ny), 1).astype(F32) - y)
    out_ref[...] = jnp.exp2(scale[:, :1] - gap * rate[:, :1]).astype(BF16)


def near_body(
    ny_loc,
    nx,
    length_x_ref,
    length_y_ref,
    own_ref,
    far_ref,
    base_ref,
    out_ref,
    moments_ref,
    rounds_ref,
    obs_ref,
    total_ref,
    count_ref,
    scalar_ref,
    a_ref,
):
    srcs = own_ref.shape[0]
    members, _, cols, ny = out_ref.shape
    level = pl.program_id(0)
    lane = iota((KEPT, CAP), 1)
    last = iota((KEPT, CAP), 0) == KEPT - 1

    @pl.when(level == 0)
    def _():
        most = counts = jnp.zeros((8, CAP), F32)
        for which, ref in enumerate((own_ref, far_ref)):
            for src in range(srcs):
                coords = ref[src, members:KEPT, :].astype(F32)
                here = (iota((8, CAP), 1) & (HALF - 1)) == which * srcs + src
                counts = jnp.where(here, coords, counts)
                most = jnp.maximum(most, coords)
        rounds_ref[0] = jnp.max(jnp.where(iota((8, CAP), 0) == 3, most, 0.0)).astype(jnp.int32)
        count_ref[0:1, :] = counts[7:8].astype(jnp.int32)
        pltpu.sync_copy(count_ref, scalar_ref)

    for block in range(USUAL // CAP):
        obs_ref[block] = jnp.zeros((KEPT, CAP), F32)
    filled = jnp.int32(0)
    now = jnp.zeros((KEPT, CAP), F32)
    for which, ref in enumerate((own_ref, far_ref)):
        for src in range(srcs):
            count = scalar_ref[0, level * HALF + which * srcs + src]
            start = filled & (CAP - 1)
            value = jnp.where(last, float(which), ref[src].astype(F32))
            value = pltpu.roll(value, (start - level * HALF) & (CAP - 1), 1)
            valid = ((lane - start) & (CAP - 1)) < count
            now = jnp.where(valid & (lane >= start), value, now)
            obs_ref[filled >> 7] = now
            now = jnp.where(start + count >= CAP, jnp.where(valid & (lane < start), value, 0.0), now)
            filled = filled + count
    obs_ref[filled >> 7] = now
    obs_ref[(filled >> 7) + 1] = jnp.zeros((KEPT, CAP), F32)

    def constants(ref, shape):
        rate, scale = rates(jnp.full((8, CAP), ref[level], F32))
        return jnp.broadcast_to(rate[:1], shape), jnp.broadcast_to(scale[:1], shape)

    rate_x, scale_x = constants(length_x_ref, (1, CAP))
    rate_y, scale_y = constants(length_y_ref, (1, CAP))
    def build(at, blocks):
        pieces = []
        for piece, slots in enumerate(blocks):
            lanes = slice(at + piece * CAP, at + (piece + 1) * CAP)
            opposite = slots[KEPT - 1 : KEPT]
            gap = jnp.abs(iota((cols, CAP), 0).astype(F32) - slots[members + 2 : members + 3])
            gap = opposite * (nx // 2) + (1.0 - 2.0 * opposite) * gap
            filter_x = jnp.exp2(scale_x - gap * rate_x)
            for k in range(members):
                a_ref[k * cols : (k + 1) * cols, lanes] = (filter_x * slots[k : k + 1]).astype(BF16)
            row = slots[members + 1 : members + 2] - (level * ny_loc).astype(F32)
            y = slots[members : members + 1] * ny_loc + jnp.maximum(row, 0.0)
            gap = jnp.abs(iota((ny, CAP), 0).astype(F32) - y)
            pieces.append(jnp.exp2(scale_y - gap * rate_y).astype(BF16))
        size = len(blocks) * CAP
        return dot_last(a_ref[:, at : at + size], jnp.concatenate(pieces, axis=1))

    total = jnp.zeros(total_ref.shape, F32)
    for at in range(0, USUAL, WIDE):
        some = range(at // CAP, min(at + WIDE, USUAL) // CAP)
        total = total + build(at, [obs_ref[block] for block in some])
    total_ref[...] = total

    def more(i, carry):
        total_ref[...] = total_ref[...] + build(0, [obs_ref[2 * i], obs_ref[2 * i + 1]])
        return carry

    lax.fori_loop(USUAL // (2 * CAP), (filled + (2 * CAP - 1)) >> 8, more, 0)

    left, right = decays(length_x_ref[level], (cols, ny))
    for k in range(members):
        value = base_ref[k, 0].astype(F32) + total_ref[k * cols : (k + 1) * cols, :]
        out_ref[k, 0] = value
        for which, factor in enumerate((left, right, value)):
            moments_ref[which, 0, k : k + 1] = jnp.sum(value * factor, axis=0, keepdims=True)


def edge_body(cols, length_x_ref, got_ref, fy_ref, moments_ref, out_ref, sum_ref, lhs_ref):
    bands, _, lanes = got_ref.shape
    _, levels, members, ny = out_ref.shape
    rows = lanes // members
    got = [got_ref[b].astype(F32) for b in range(bands)]
    for k in range(members):
        piece = jnp.concatenate([got[b][:, k * rows : (k + 1) * rows] for b in range(bands)], axis=1)
        lhs_ref[k : k + 1, :] = piece[0:1]
        lhs_ref[members + k : members + k + 1, :] = piece[1:2]
    lhs = lhs_ref[...]
    spot = iota((1, bands * rows), 1).astype(F32) + 0.5
    level_of = (spot * (levels / rows)).astype(jnp.int32) & (levels - 1)
    lhs = jnp.concatenate([jnp.where(level_of == level, lhs, 0.0).astype(BF16) for level in range(levels)], axis=0)
    edge = jnp.dot(lhs, fy_ref[...], preferred_element_type=F32)
    total = jnp.zeros((members, ny), F32)
    for level in range(levels):
        at = 2 * level * members
        one, two = edge[at : at + members], edge[at + members : at + 2 * members]
        out_ref[0, level], out_ref[1, level] = one, two
        left, right = decays(length_x_ref[level], (cols, 128))

        def over_columns(value):
            return jnp.sum(value, axis=0, keepdims=True)[:, :1]

        total = total + moments_ref[2, level]
        total = total + one * (2.0 * moments_ref[0, level] + one * over_columns(left * left))
        total = total + two * (2.0 * moments_ref[1, level] + two * over_columns(right * right))
        total = total + one * two * (2.0 * over_columns(left * right))
    sum_ref[...] = jnp.full(sum_ref.shape, jnp.sum(total), F32)


def final_body(length_x_ref, edge_ref, near_ref, out_ref):
    part, levels, cols, ny = out_ref.shape
    for level in range(levels):
        left, right = decays(length_x_ref[level], (cols, ny))
        for k in range(part):
            one, two = edge_ref[0, level, k : k + 1], edge_ref[1, level, k : k + 1]
            out_ref[k, level] = near_ref[k, level] + left * one + right * two


def on_device(control, member_pert, obs_weight, obs_band, obs_cell, length_x, length_y):
    members, levels, x_block, ny = control.shape
    bands = lax.axis_size("band")
    groups = lax.axis_size("mem")
    ny_loc = ny // bands
    nx = x_block * bands
    obs = obs_cell.shape[0]
    rows = levels * ny_loc
    size = 2 * (KEPT - members)

    def route(turn, beside=None):
        packed = pl.pallas_call(
            lambda *refs: bucket_body(nx, rows, x_block, *refs),
            in_specs=[SMEM] + [pl.BlockSpec(memory_space=pltpu.VMEM)] * 4,
            out_shape=jax.ShapeDtypeStruct((bands, KEPT + members, CAP), BF16),
            scratch_shapes=[
                pltpu.VMEM((8, obs), jnp.int32),
                pltpu.VMEM((members + size, obs), BF16),
                pltpu.VMEM((bands * KEPT, obs), BF16),
            ],
            compiler_params=room(16),
            name="bucket",
        )(turn, obs_band.reshape(1, obs), obs_cell.reshape(1, obs), obs_weight.reshape(1, obs), member_pert)
        got = lax.all_to_all(packed, "band", 0, 0, tiled=True)
        if beside is not None:
            got, beside = lax.optimization_barrier((got, beside))
        own = got[:, :KEPT]
        swap = [(i, (i + bands // 2) % bands) for i in range(bands)]
        return got, own, lax.ppermute(own, "band", swap), beside

    def near_field(own, opposite, base):
        by_level = pl.BlockSpec((members, 1, x_block, ny), lambda i: (0, i, 0, 0))
        slots = 2 * bands * HALF
        return pl.pallas_call(
            lambda *refs: near_body(ny_loc, nx, *refs),
            grid=(levels,),
            in_specs=[
                SMEM,
                SMEM,
                pl.BlockSpec((bands, KEPT, CAP), lambda i: (0, 0, 0)),
                pl.BlockSpec((bands, KEPT, CAP), lambda i: (0, 0, 0)),
                by_level,
            ],
            out_specs=[by_level, pl.BlockSpec((3, 1, members, ny), lambda i: (0, i, 0, 0)), SMEM],
            out_shape=[
                jax.ShapeDtypeStruct((members, levels, x_block, ny), F32),
                jax.ShapeDtypeStruct((3, levels, members, ny), F32),
                jax.ShapeDtypeStruct((1,), jnp.int32),
            ],
            scratch_shapes=[
                pltpu.VMEM((slots // CAP + 8, KEPT, CAP), F32),
                pltpu.VMEM((members * x_block, ny), F32),
                pltpu.VMEM((1, CAP), jnp.int32),
                pltpu.SMEM((1, CAP), jnp.int32),
                pltpu.VMEM((members * x_block, USUAL), BF16),
            ],
            compiler_params=room(52),
            cost_estimate=pl.CostEstimate(
                flops=levels * members * x_block * slots * ny, bytes_accessed=8_000_000, transcendentals=4_000_000
            ),
            name="near",
        )(length_x, length_y, own, opposite, base)

    some = 8 * rows
    filter_y = pl.pallas_call(
        lambda *refs: filter_body(rows, *refs),
        grid=(bands * rows // some,),
        in_specs=[SMEM],
        out_specs=pl.BlockSpec((some, ny), lambda i: (i, 0)),
        out_shape=jax.ShapeDtypeStruct((bands * rows, ny), BF16),
        compiler_params=room(16),
        cost_estimate=pl.CostEstimate(flops=5_000_000, bytes_accessed=3_000_000, transcendentals=1_200_000),
        name="filter",
    )(length_y)

    got, own, opposite, filter_y = route(jnp.zeros((1,), jnp.int32), filter_y)
    states = pl.pallas_call(
        lambda *refs: states_body(rows, x_block, *refs),
        in_specs=[SMEM, pl.BlockSpec(memory_space=pltpu.VMEM)],
        out_shape=jax.ShapeDtypeStruct((bands, 2, members * rows), BF16),
        scratch_shapes=[pltpu.VMEM((members * rows, bands * CAP), BF16), pltpu.VMEM((8, bands * CAP), F32)],
        compiler_params=room(20),
        name="states",
    )(length_x, got)
    edges = lax.all_to_all(states, "band", 0, 0, tiled=True)

    near, moments, rounds = near_field(own, opposite, control)

    def again(carry):
        turn, near, _ = carry
        _, more, more_opposite, _ = route(turn.reshape(1))
        return (turn + 1, *near_field(more, more_opposite, near)[:2])

    _, near, moments = lax.while_loop(lambda carry: carry[0] < rounds[0], again, (jnp.int32(1), near, moments))

    edge, partial_value = pl.pallas_call(
        lambda *refs: edge_body(x_block, *refs),
        in_specs=[SMEM] + [pl.BlockSpec(memory_space=pltpu.VMEM)] * 3,
        out_shape=[
            jax.ShapeDtypeStruct((2, levels, members, ny), F32),
            jax.ShapeDtypeStruct((groups * bands, 128), F32),
        ],
        scratch_shapes=[pltpu.VMEM((2 * members, bands * rows), F32)],
        compiler_params=room(16),
        name="edge",
    )(length_x, edges, filter_y, moments)
    partials = lax.all_to_all(partial_value, ("mem", "band"), 0, 0, tiled=True)

    part = 8
    by_member = pl.BlockSpec((part, levels, x_block, ny), lambda i: (i, 0, 0, 0))
    gradient = pl.pallas_call(
        final_body,
        grid=(members // part,),
        in_specs=[SMEM, pl.BlockSpec((2, levels, part, ny), lambda i: (0, 0, i, 0)), by_member],
        out_specs=by_member,
        out_shape=jax.ShapeDtypeStruct((members, levels, x_block, ny), F32),
        compiler_params=room(24),
        cost_estimate=pl.CostEstimate(flops=20_000_000, bytes_accessed=10_000_000, transcendentals=0),
        name="final",
    )(length_x, edge, near)
    gradient_dot = jnp.sum(partials[:, 0]) * (1.0 / (members * groups * levels * ny * nx))
    return (gradient, gradient_dot)


def solution(mesh):
    return jax.shard_map(
        on_device,
        mesh=mesh,
        in_specs=(
            P("mem", None, "band", None),
            P("mem", "band"),
            P("band"),
            P("band", None),
            P("band"),
            P(),
            P(),
        ),
        out_specs=(P("mem", None, "band", None), P()),
        check_vma=False,
    )
```
